512 devices in a mesh: band: 16 (over z, core), tile: 32 (over x, y).
Axes of the slice: x: 4, y: 8, z: 8, core: 2. Of those that a mesh axis runs over, the one named last changes fastest.
Arguments:
- displacement: float32 [3, 128, 512, 512], P(None, 'band', 'tile'), may hold values from -3 to 3
- old_mass: float32 [262144, 128], P(('band', 'tile')), may hold values from 0.5 to 2
- old_momentum: float32 [262144, 3, 128], P(('band', 'tile')), may hold values from -6 to 6
- intersection_fraction: float32 [262144, 128], P(('band', 'tile')), may hold values from 0.1 to 0.9
- entry_order: int32 [512, 1024], P(('band', 'tile')), may hold values from 0 to 1023, each once within a row
- target_owner: int32 [524288, 1], P(('band', 'tile')), may hold values from 0 to 31; in each aligned block of 1024 rows (0 to 1023, 1024 to 2047, ...) at most 40 rows name the same one
- target_block: int32 [524288], P(('band', 'tile')), may hold values from 0 to 511
- kept_mass: float32 [128, 512, 512], P('band', 'tile'), may hold values from 0.5 to 2
- kept_momentum: float32 [3, 128, 512, 512], P(None, 'band', 'tile'), may hold values from -6 to 6
- surface_panels: float32 [2048, 3, 128], P(('band', 'tile')), may hold values from -6 to 6
- panel_ids: int32 [16, 512, 4], P('band', 'tile'), may hold values from 0 to 127
- contact_flags: int32 [16, 512, 4], P('band', 'tile'), may hold values 0 or 1
Outputs:
- regridded: float32 [3, 128, 512, 512], P(None, 'band', 'tile')
- velocity: float32 [3, 128, 512, 512], P(None, 'band', 'tile')
The draws below stay inside these ranges and needn't reach their ends.
Inputs may be any that keep to these rules, and one draw needn't show every extreme that they name: `entry_order`: each device's row is a permutation of 0 to 1023. `target_owner`: among the 1024 entries of one device no owner is named more than 40 times, a bound that some block reaches.
All inputs are finite; a program needn't handle non-finite values. No bound on the sum of `contact_flags` on one device may be relied on, other than what follows from the above.
Results may differ from the reference program's by a relative error of at most 0.0003.
Values sent between devices are 32-bit elements; how exact they have to be, the bound alone decides.
A program may use at most 64 MiB of HBM per device.

```python
import math
import jax
import jax.numpy as jnp
import numpy as np
from jax import lax

CZ = 8
CX = 16
CY = 512
PAN_DEV = 4
ITERS_W = 2
NZ = 128
NX = 512
NYB = 4
NBLK = 512
OV = 1024
CAP = 40
N_BAND = 16
N_TILE = 32
DEVICES = 512


def plant(values, rng, low, high):
    place = [jax.random.randint(jax.random.fold_in(rng, axis), (), 0, length) for axis, length in enumerate(values.shape)]
    longest = values.shape.index(max(values.shape))
    beside = place[:longest] + [(place[longest] + 1) % values.shape[longest]] + place[longest + 1:]
    return values.at[tuple(place)].set(low).at[tuple(beside)].set(high)


def block_scale(own_key, dims, cuts, low, top_value):
    level = 1.0
    for dim, blocks in cuts:
        draws = jax.random.uniform(jax.random.fold_in(jax.random.fold_in(own_key, 6), dim), (blocks,), jnp.float32, low / len(cuts), top_value / len(cuts))
        level = level * jnp.repeat(jnp.exp(draws), dims[dim] // blocks).reshape((-1,) + (1,) * (len(dims) - 1 - dim))
    return level


def assign_block(rng, own, number, rows, count, top, limit, lean):
    ranking = jax.random.permutation(rng, count)
    heavy_load, ordinary = portions_of(count, rows * top, limit, lean, True), portions_of(count, rows * top, limit, lean, False)
    places = jnp.arange(count)

    def named(lengths, rotation):
        used = int((lengths > 0).sum())
        fixed = max(1, used // 4)
        passed = fixed + (places - fixed + rotation * (used - fixed)) % max(1, count - fixed)
        return jnp.zeros((count,), jnp.int32).at[ranking[jnp.where(places < fixed, places, passed)]].set(jnp.asarray(lengths, jnp.int32))

    lengths = jnp.where(number % 4 == 0, named(heavy_load, number // 4), named(ordinary, number - number // 4 - 1))
    mixed = jax.random.permutation(jax.random.fold_in(own, 3), count)
    source_of, sink = mixed[0:count // 2 * 2:2], mixed[1:count // 2 * 2:2]
    margin = jnp.minimum(lengths[source_of] - 1, limit - lengths[sink]) // 2
    margin = jnp.where((source_of == ranking[0]) | (sink == ranking[0]) | (lengths[sink] == 0), 0, jnp.maximum(margin, 0))
    passed = jax.random.randint(jax.random.fold_in(own, 4), (count // 2,), 0, 1 << 20) % (margin + 1)
    lengths = lengths.at[source_of].add(-passed).at[sink].add(passed)
    members = jnp.searchsorted(jnp.cumsum(lengths), jnp.arange(rows * top), side="right").astype(jnp.int32)
    listing = members.reshape(top, rows).T
    listing = listing[jax.random.permutation(jax.random.fold_in(own, 1), rows)]
    rotation = jax.random.randint(jax.random.fold_in(own, 2), (rows, 1), 0, top)
    return jnp.take_along_axis(listing, (jnp.arange(top)[None, :] + rotation) % top, axis=1)


def portions_of(count, total, bound, slope, full):
    portions = [(1 << 20) // math.isqrt(grade ** slope) + 1 for grade in range(1, count + 1)]
    largest = bound if full else min(bound, max(-(-total // count), total * portions[0] // sum(portions)))
    least = 1 if total - largest >= count - 1 else 0
    counts, surplus = [largest] + [least] * (count - 1), total - largest - least * (count - 1)
    while surplus > 0:
        candidates = [i for i in range(1, count) if counts[i] < largest] or [i for i in range(1, count) if counts[i] < bound]
        whole, remaining = sum([portions[i] for i in candidates]), surplus
        for i in candidates:
            extra = min(bound - counts[i], max(1, remaining * portions[i] // whole), surplus)
            counts[i] = counts[i] + extra
            surplus = surplus - extra
    return np.array(counts)


def normal_values(stream_key, shape, deviation, reach, split=(), held_as=jnp.bfloat16):
    values = deviation * jax.random.normal(stream_key, shape, jnp.float32)
    if split:
        values = values * block_scale(stream_key, shape, split, -0.22, 0.18)
    return jnp.clip(values, -reach, reach).astype(held_as)


def setup_inputs(seed: int = 0) -> dict:
    seeds = jax.random.split(jax.random.key(seed), 13)
    displacement = normal_values(seeds[0], (3, NZ, NX, CY), 0.5, 3.0, ((1, 16), (2, 32)), jnp.float32)
    old_mass = jnp.clip(jnp.exp(math.log(2.0) - 1.3862944 * jax.random.uniform(seeds[1], (DEVICES * NBLK, 128), jnp.float32) ** block_scale(seeds[1], (DEVICES * NBLK, 128), ((0, 512),), -0.2, 0.2)), 0.5, 2.0)
    old_momentum = normal_values(seeds[2], (DEVICES * NBLK, 3, 128), 1.0, 6.0, ((0, 512),), jnp.float32)
    intersection_fraction = jnp.clip(0.1 + 0.79999997 * jax.random.uniform(seeds[3], (DEVICES * NBLK, 128), jnp.float32) ** block_scale(seeds[3], (DEVICES * NBLK, 128), ((0, 512),), -0.2, 0.2), 0.1, 0.9)
    entry_order = jax.vmap(lambda own: jax.random.permutation(own, OV))(jax.random.split(seeds[4], DEVICES)).reshape((DEVICES, OV)).astype(jnp.int32)
    target_owner_keys = jax.random.split(jax.random.fold_in(seeds[5], 1), (DEVICES * OV) // OV)
    target_owner_turns = jax.random.permutation(jax.random.fold_in(seeds[5], 3), (DEVICES * OV) // OV)
    target_owner = jax.vmap(lambda own, number: assign_block(jax.random.fold_in(seeds[5], 2), own, number, OV, N_TILE, 1, CAP, 2))(target_owner_keys, target_owner_turns).reshape((DEVICES * OV, 1))
    target_block = plant(jax.random.randint(seeds[6], (DEVICES * OV,), 0, NBLK), jax.random.fold_in(seeds[6], 1), 0, NBLK - 1).astype(jnp.int32)
    kept_mass = jnp.clip(jnp.exp(math.log(2.0) - 1.3862944 * jax.random.uniform(seeds[7], (NZ, NX, CY), jnp.float32) ** block_scale(seeds[7], (NZ, NX, CY), ((0, 16), (1, 32)), -0.2, 0.2)), 0.5, 2.0)
    kept_momentum = normal_values(seeds[8], (3, NZ, NX, CY), 1.0, 6.0, ((1, 16), (2, 32)), jnp.float32)
    surface_panels = normal_values(seeds[9], (DEVICES * PAN_DEV, 3, 128), 1.0, 6.0, ((0, 512),), jnp.float32)
    panel_ids = plant(jax.random.randint(seeds[10], (N_BAND, NX, NYB), 0, PAN_DEV * N_TILE), jax.random.fold_in(seeds[10], 1), 0, (PAN_DEV * N_TILE) - 1).astype(jnp.int32)
    contact_flags = plant((jax.random.randint(seeds[11], (N_BAND, NX, NYB), 0, 2) < 1).astype(jnp.int32), jax.random.fold_in(seeds[11], 1), 0, 1)
    return {"displacement": displacement, "old_mass": old_mass, "old_momentum": old_momentum, "intersection_fraction": intersection_fraction, "entry_order": entry_order, "target_owner": target_owner, "target_block": target_block, "kept_mass": kept_mass, "kept_momentum": kept_momentum, "surface_panels": surface_panels, "panel_ids": panel_ids, "contact_flags": contact_flags}


relax_factor = 0.8
cell_fraction = 0.1
strain_eps = 0.05
rate_power = -0.4
penalty_factor = 0.5


def ahead(grid_field, dimension):
    padding = [(0, 0)] * grid_field.ndim
    padding[dimension] = (0, 1)
    extent = grid_field.shape[dimension]
    return lax.slice_in_dim(jnp.pad(grid_field, padding), 1, extent + 1, axis=dimension)


def behind(grid_field, dimension):
    padding = [(0, 0)] * grid_field.ndim
    padding[dimension] = (1, 0)
    extent = grid_field.shape[dimension]
    return lax.slice_in_dim(jnp.pad(grid_field, padding), 0, extent, axis=dimension)


def remap_band(pieces):
    order_band, owner_band, block_band, mass_band, momentum_band, fraction_band = pieces
    source = order_band // 2
    fraction = jnp.take_along_axis(fraction_band, source[:, :, None], axis=1)
    weights = jnp.where((order_band % 2 == 0)[:, :, None], fraction, 1.0 - fraction)
    moved_mass = weights * jnp.take_along_axis(mass_band, source[:, :, None], axis=1)
    moved_momentum = weights[:, :, None, :] * jnp.take_along_axis(momentum_band, source[:, :, None, None], axis=1)
    segment = (owner_band * NBLK + block_band).reshape(-1)
    in_mass = jax.ops.segment_sum(moved_mass.reshape(-1, 128), segment, num_segments=N_TILE * NBLK)
    in_momentum = jax.ops.segment_sum(moved_momentum.reshape(-1, 3, 128), segment, num_segments=N_TILE * NBLK)
    in_mass = in_mass.reshape(N_TILE, CZ, CX, CY).transpose(1, 0, 2, 3).reshape(CZ, NX, CY)
    in_momentum = in_momentum.reshape(N_TILE, NBLK, 3, 128).transpose(2, 0, 1, 3)
    in_momentum = in_momentum.reshape(3, N_TILE, CZ, CX, CY).transpose(0, 2, 1, 3, 4).reshape(3, CZ, NX, CY)
    return in_mass, in_momentum


def pick_panels(band_panels, band_ids):
    return band_panels[band_ids]


def reference(displacement, old_mass, old_momentum, intersection_fraction, entry_order, target_owner, target_block, kept_mass, kept_momentum, surface_panels, panel_ids, contact_flags):
    regridded = displacement
    for sweep_index in range(ITERS_W):
        neighbours = jnp.zeros_like(regridded)
        for dimension in (1, 2, 3):
            neighbours = neighbours + ahead(regridded, dimension) + behind(regridded, dimension)
        regridded = regridded + relax_factor * (neighbours / 6.0 - regridded)
    stretch = jnp.zeros_like(regridded[0])
    for component in range(3):
        stretch = stretch + 0.5 * (ahead(regridded[component], component) - behind(regridded[component], component))
    volume = 1.0 + cell_fraction * stretch

    pieces = (entry_order.reshape(N_BAND, N_TILE, OV), target_owner.reshape(N_BAND, N_TILE, OV),
              target_block.reshape(N_BAND, N_TILE, OV), old_mass.reshape(N_BAND, N_TILE, NBLK, 128),
              old_momentum.reshape(N_BAND, N_TILE, NBLK, 3, 128), intersection_fraction.reshape(N_BAND, N_TILE, NBLK, 128))
    in_mass, in_momentum = lax.map(remap_band, pieces)
    in_mass = in_mass.reshape(NZ, NX, CY)
    in_momentum = in_momentum.transpose(1, 0, 2, 3, 4).reshape(3, NZ, NX, CY)
    mass = kept_mass + in_mass
    momentum = kept_momentum + in_momentum
    speed = momentum / mass[None]
    density = mass / volume

    band_panels = surface_panels.reshape(N_BAND, N_TILE * PAN_DEV, 3, 128)
    picked = jax.vmap(pick_panels)(band_panels, panel_ids)
    picked = picked * contact_flags.astype(jnp.float32)[:, :, :, None, None]
    traction = picked.transpose(3, 0, 1, 2, 4).reshape(3, N_BAND, NX, CY)
    traction = jnp.repeat(traction, CZ, axis=1)

    squares = jnp.zeros_like(mass)
    for component in range(3):
        for dimension in range(3):
            change = ahead(speed[component], dimension) - speed[component]
            squares = squares + change * change
    viscous = (strain_eps + squares) ** rate_power
    divergence = jnp.zeros_like(mass)
    for component in range(3):
        divergence = divergence + (speed[component] - behind(speed[component], component))
    pressure = -penalty_factor * divergence

    face_sum = jnp.zeros_like(mass)
    fluxes = [jnp.zeros_like(mass) for component in range(3)]
    for dimension in range(3):
        forward_face = 0.5 * (viscous + ahead(viscous, dimension))
        backward_face = 0.5 * (viscous + behind(viscous, dimension))
        face_sum = face_sum + forward_face + backward_face
        for component in range(3):
            fluxes[component] = fluxes[component] + forward_face * ahead(speed[component], dimension) + backward_face * behind(speed[component], dimension)
    denominator = face_sum + density
    results = []
    for component in range(3):
        gradient = ahead(pressure, component) - pressure
        numerator = fluxes[component] - gradient + traction[component] + density * speed[component]
        results.append(numerator / denominator)
    return regridded, jnp.stack(results)
```

```python
import jax
import jax.numpy as jnp
from jax import lax
from jax.experimental import pallas as pl
from jax.experimental.pallas import tpu as pltpu
from jax.sharding import PartitionSpec as P

MESH = pl.DeviceIdType.MESH
F32, BF16 = jnp.float32, jnp.bfloat16

relax_factor = 0.8
cell_fraction = 0.1
strain_eps = 0.05
rate_power = -0.4
penalty_factor = 0.5

N_BAND, N_TILE = 16, 32
TX, TY = 4, 8
CZ, CX, CY = 8, 16, 512
OV, NBLK, CAP = 1024, 512, 40
COMPS = 4
GROUP = 4
GROUPS = N_TILE // GROUP
ROWS = GROUP * CAP
SETS = (N_TILE + 2) // 3
RROWS = SETS * 128
TOP = 8


def slot_row(k):
    return 128 * (k // 3) + CAP * (k % 3)


def split2(value):
    high = value.astype(BF16)
    low = (value - high.astype(F32)).astype(BF16)
    return high, low


def iota(shape, dim):
    return lax.broadcasted_iota(jnp.int32, shape, dim)


def ahead_y(f):
    n = f.shape[-1]
    return jnp.where(iota(f.shape, f.ndim - 1) == n - 1, 0.0, pltpu.roll(f, n - 1, f.ndim - 1))


def behind_y(f):
    return jnp.where(iota(f.shape, f.ndim - 1) == 0, 0.0, pltpu.roll(f, 1, f.ndim - 1))


def ahead_x(f, row):
    n = f.shape[0]
    return jnp.where(iota(f.shape, 0) == n - 1, row, pltpu.roll(f, n - 1, 0))


def behind_x(f, row):
    return jnp.where(iota(f.shape, 0) == 0, row, pltpu.roll(f, 1, 0))


def visc_of(squares):
    return jnp.exp(rate_power * jnp.log(strain_eps + squares))


def kernel(
    disp_hbm, mass_hbm, mom_hbm, frac_hbm, order_ref, owner_ref, block_ref,
    kmass_hbm, kmom_hbm, panels_ref, pids_ref, flags_ref,
    regrid_hbm, vel_ref,
    ext, s1, old, frac, kmass, kmom, vol, sel_src, table, send, recv, ids_send, ids_recv,
    sel_dst, xst, xhl, xhr, cst, chl, pans, trac, spd, plane, xm1, xp16, xp17, visc, pres,
    load_sem, out_sem, a2a_send, a2a_recv, ids_ssem, ids_rsem, dh_send, dh_recv,
    py_send, py_recv, px_send, px_recv, sp_send, sp_recv,
):
    b = lax.axis_index("band")
    t = lax.axis_index("tile")
    tx, ty = t // TY, t % TY
    up, down = (b + 1) % N_BAND, (b + N_BAND - 1) % N_BAND
    right, left = (t + 1) % N_TILE, (t + N_TILE - 1) % N_TILE

    def peer(k):
        return ((tx + k // TY) % TX) * TY + (ty + k % TY) % TY

    barrier = pltpu.get_barrier_semaphore()
    partners = [(b, peer(k)) for k in range(1, N_TILE)]
    partners += [(up, t), (down, t), (up, right), (up, left), (down, right), (down, left)]
    for partner in partners:
        pl.semaphore_signal(barrier, inc=1, device_id=partner, device_id_type=MESH)

    loads = [
        pltpu.make_async_copy(disp_hbm, ext.at[:, pl.ds(3, CZ), pl.ds(TOP, CX), :], load_sem.at[0]),
        pltpu.make_async_copy(frac_hbm, frac, load_sem.at[1]),
        pltpu.make_async_copy(mass_hbm, old.at[0], load_sem.at[2]),
        pltpu.make_async_copy(mom_hbm, old.at[pl.ds(1, 3)], load_sem.at[3]),
        pltpu.make_async_copy(kmass_hbm, kmass, load_sem.at[4]),
        pltpu.make_async_copy(kmom_hbm, kmom, load_sem.at[5]),
    ]
    for copy in loads:
        copy.start()

    owner = owner_ref[...]
    column = iota((N_TILE, 1), 0)
    column_dest = ((tx + column // TY) % TX) * TY + (ty + column % TY) % TY
    before = (iota((128, 128), 0) < iota((128, 128), 1)).astype(BF16)
    base = jnp.zeros((N_TILE, 1), F32)
    slots, names = [], []
    for j in range(OV // 128):
        hot = (owner[:, 128 * j : 128 * (j + 1)] == column_dest).astype(F32)
        prefix = base + jnp.dot(hot.astype(BF16), before, preferred_element_type=F32)
        slots.append(jnp.sum(hot * prefix, axis=0, keepdims=True))
        names.append(jnp.sum(hot * column.astype(F32), axis=0, keepdims=True))
        base = base + jnp.sum(hot, axis=1, keepdims=True)
    slot = jnp.concatenate(slots, axis=1)
    name = jnp.concatenate(names, axis=1)
    place = name * CAP + slot
    order = order_ref[...]
    code = (order // 2 + (order % 2) * NBLK + 1).astype(F32)

    block = block_ref[...]
    target = (block % 4) * 128 + block // 4 + 1
    hot = owner == column_dest
    high = jnp.where(hot, target // 16, 0).astype(F32).astype(BF16)
    low = jnp.where(hot, target % 16, 0).astype(F32).astype(BF16)
    lanes = (slot == iota((128, 1), 0).astype(F32)).astype(F32).astype(BF16)
    dims = (((1,), (1,)), ((), ()))
    ids = 16.0 * lax.dot_general(high, lanes, dims, preferred_element_type=F32)
    ids = ids + lax.dot_general(low, lanes, dims, preferred_element_type=F32)
    third = iota((N_TILE, 128), 0) % 3
    ids = jnp.where(
        third == 0, ids, jnp.where(third == 1, pltpu.roll(ids, CAP, 1), pltpu.roll(ids, 2 * CAP, 1))
    )
    for k in range(N_TILE):
        ids_send[k] = ids[k : k + 1, :]
    ids_recv[0] = ids[0:1, :]

    loads[0].wait()
    for c in range(3):
        for k in range(3):
            at = pl.ds(24 * c + 8 * k, 8)
            xst[0, at, :] = ext[c, 3:11, TOP + 13 + k, :]
            xst[1, at, :] = ext[c, 3:11, TOP + k, :]
    for corner in range(4):
        sz, sx = corner // 2, corner % 2
        for c in range(3):
            for i, (dz, dx) in enumerate(((1, 1), (1, 2), (2, 1))):
                z = CZ - dz if sz else dz - 1
                x = CX - dx if sx else dx - 1
                cst[corner, pl.ds(3 * c + i, 1), :] = ext[c, 3 + z, pl.ds(TOP + x, 1), :]
    pans[ty] = panels_ref[...]

    pl.semaphore_wait(barrier, len(partners))

    def remote(src, dst, ssem, rsem, device):
        return pltpu.make_async_remote_copy(
            src_ref=src, dst_ref=dst, send_sem=ssem, recv_sem=rsem, device_id=device, device_id_type=MESH
        )

    disp_copies = [
        remote(xst.at[0], xhl, dh_send.at[0], dh_recv.at[0], (b, right)),
        remote(xst.at[1], xhr, dh_send.at[1], dh_recv.at[1], (b, left)),
        remote(disp_hbm.at[:, pl.ds(CZ - 3, 3)], ext.at[:, pl.ds(0, 3), pl.ds(TOP, CX), :],
               dh_send.at[2], dh_recv.at[2], (up, t)),
        remote(disp_hbm.at[:, pl.ds(0, 3)], ext.at[:, pl.ds(3 + CZ, 3), pl.ds(TOP, CX), :],
               dh_send.at[3], dh_recv.at[3], (down, t)),
    ]
    for corner in range(4):
        sz, sx = corner // 2, corner % 2
        disp_copies.append(
            remote(cst.at[corner], chl.at[corner], dh_send.at[4 + corner], dh_recv.at[4 + corner],
                   (up if sz else down, right if sx else left))
        )
    for copy in disp_copies:
        copy.start()
    panel_y = [
        remote(pans.at[ty], pans.at[ty], py_send.at[i - 1], py_recv.at[i - 1], (b, tx * TY + (ty + i) % TY))
        for i in range(1, TY)
    ]
    for copy in panel_y:
        copy.start()

    ids_copies = [
        remote(ids_send.at[k], ids_recv.at[k], ids_ssem, ids_rsem, (b, peer(k))) for k in range(1, N_TILE)
    ]

    for copy in loads[1:4]:
        copy.wait()

    def fill_table(c):
        share = frac[...]
        values = old[c]
        one = share * values
        high, low = split2(one)
        table[0:NBLK, 0:128] = high
        table[0:NBLK, 128:256] = low
        high, low = split2((1.0 - share) * values)
        table[NBLK : 2 * NBLK, 0:128] = high
        table[NBLK : 2 * NBLK, 128:256] = low

    def rows_copy(c, k):
        return remote(
            send.at[c, pl.ds(CAP * k, CAP), :], recv.at[c, pl.ds(slot_row(k), CAP), :],
            a2a_send.at[c], a2a_recv.at[c], (b, peer(k)),
        )

    def dispatch(c, g):
        both = jnp.dot(sel_src[g], table[...], preferred_element_type=F32)
        rows = both[:, 0:128] + both[:, 128:256]
        send[c, pl.ds(ROWS * g, ROWS), :] = rows
        if g == 0:
            recv[c, 0:CAP, :] = rows[0:CAP]
        for j in range(GROUP):
            k = GROUP * g + j
            if k:
                rows_copy(c, k).start()

    fill_table(0)
    for g in range(GROUPS):
        wanted = (ROWS * g + iota((ROWS, 1), 0)).astype(F32)
        code_of = jnp.sum(jnp.where(place == wanted, code, 0.0), axis=1, keepdims=True)
        hit = code_of.astype(jnp.int32) == iota((ROWS, OV), 1) + 1
        sel_src[g] = jnp.where(hit, 1.0, 0.0).astype(BF16)
        dispatch(0, g)
        if g == 0:
            for copy in ids_copies:
                copy.start()

    for i, copy in enumerate(panel_y):
        copy.wait()

    panel_x = [
        remote(pans.at[pl.ds(0, TY)], pans.at[pl.ds(TY * i, TY)], px_send.at[i - 1], px_recv.at[i - 1],
               (b, ((tx + i) % TX) * TY + ty))
        for i in range(1, TX)
    ]
    for copy in panel_x:
        copy.start()

    def later(c, carry):
        fill_table(c)
        for g in range(GROUPS):
            dispatch(c, g)
        return carry

    lax.fori_loop(1, COMPS, later, 0)

    for copy in disp_copies:
        copy.wait()
    at_left, at_right = t == 0, t == N_TILE - 1
    at_bottom, at_top = b == 0, b == N_BAND - 1
    nothing = jnp.zeros((8, CY), F32)
    for c in range(3):
        for k in range(3):
            at = pl.ds(24 * c + 8 * k, 8)
            ext[c, 3:11, TOP - 3 + k, :] = jnp.where(at_left, nothing, xhl[at, :])
            ext[c, 3:11, TOP + CX + k, :] = jnp.where(at_right, nothing, xhr[at, :])

    @pl.when(at_bottom)
    def _():
        ext[:, 0:3, TOP : TOP + CX, :] = jnp.zeros((3, 3, CX, CY), F32)

    @pl.when(at_top)
    def _():
        ext[:, 3 + CZ : 6 + CZ, TOP : TOP + CX, :] = jnp.zeros((3, 3, CX, CY), F32)

    for corner in range(4):
        sz, sx = corner // 2, corner % 2
        outside = (at_bottom if sz else at_top) | (at_left if sx else at_right)
        for c in range(3):
            for i, (dz, dx) in enumerate(((1, 1), (1, 2), (2, 1))):
                z = -dz if sz else CZ - 1 + dz
                x = -dx if sx else CX - 1 + dx
                line = chl[corner, pl.ds(3 * c + i, 1), :]
                ext[c, 3 + z, pl.ds(TOP + x, 1), :] = jnp.where(outside, jnp.zeros_like(line), line)

    row = iota((32, CY), 0) - TOP
    keep_x = ((row >= 0) | jnp.logical_not(at_left)) & ((row < CX) | jnp.logical_not(at_right))

    def sweep(src, dst, c, zi):
        here = src[c, zi]
        near = src[c, zi + 1] + src[c, zi - 1]
        near = near + pltpu.roll(here, 1, 0) + pltpu.roll(here, 31, 0)
        near = near + ahead_y(here) + behind_y(here)
        new = here + relax_factor * (near / 6.0 - here)
        z = zi - 3
        inside = ((z >= 0) | jnp.logical_not(at_bottom)) & ((z < CZ) | jnp.logical_not(at_top))
        dst[c, zi] = jnp.where(keep_x & inside, new, 0.0)

    def first(zi, carry):
        for c in range(3):
            sweep(ext, s1, c, zi)
        return carry

    def second(zi, carry):
        for c in range(3):
            sweep(s1, ext, c, zi)
        return carry

    lax.fori_loop(1, 13, first, 0)
    lax.fori_loop(2, 12, second, 0)
    regrid_out = pltpu.make_async_copy(
        ext.at[:, pl.ds(3, CZ), pl.ds(TOP, CX), :], regrid_hbm, out_sem.at[0]
    )
    regrid_out.start()

    def volumes(z, carry):
        zi = z + 3
        own = pl.ds(TOP, CX)
        stretch = ext[0, zi + 1, own, :] - ext[0, zi - 1, own, :]
        across = ext[1, zi]
        across = pltpu.roll(across, 31, 0) - pltpu.roll(across, 1, 0)
        along = ext[2, zi, own, :]
        stretch = stretch + across[TOP : TOP + CX] + (ahead_y(along) - behind_y(along))
        vol[z] = 1.0 + cell_fraction * (0.5 * stretch)
        return carry

    lax.fori_loop(0, CZ, volumes, 0)

    for copy in panel_x:
        copy.wait()
    source = iota((N_TILE * 4, CX), 0)
    member = source // 4
    panel = ((tx + TX - member // TY) % TX) * (TY * 4) + (member % TY) * 4 + source % 4
    for yb in range(CY // 128):
        chosen = (panel == pids_ref[yb : yb + 1, :]) & (flags_ref[yb : yb + 1, :] != 0)
        chosen = jnp.where(chosen, 1.0, 0.0)
        for c in range(3):
            faces = pans[:, c].reshape(N_TILE * 4, 128)
            high, low = split2(faces)
            tn = (((0,), (0,)), ((), ()))
            weight = chosen.astype(BF16)
            got = lax.dot_general(weight, high, tn, preferred_element_type=F32)
            got = got + lax.dot_general(weight, low, tn, preferred_element_type=F32)
            trac[c, :, 128 * yb : 128 * (yb + 1)] = got

    bulk = (N_TILE - 1) * CAP
    pltpu.make_async_copy(ids_recv.at[pl.ds(1, N_TILE - 1)], ids_recv.at[pl.ds(1, N_TILE - 1)], ids_rsem).wait()
    number = iota((NBLK, 128), 0).astype(F32) + 1.0
    for s in range(SETS):
        line = ids_recv[3 * s]
        for k in range(3 * s + 1, min(3 * s + 3, N_TILE)):
            line = line + ids_recv[k]
        sel_dst[:, 128 * s : 128 * (s + 1)] = jnp.where(number == line, 1.0, 0.0).astype(BF16)
    for s in range(SETS):
        used = CAP * min(3, N_TILE - 3 * s)
        for c in range(COMPS):
            recv[c, 128 * s + used : 128 * (s + 1), :] = jnp.zeros((128 - used, 128), F32)

    def incoming(c):
        pltpu.make_async_copy(recv.at[c, pl.ds(0, bulk)], recv.at[c, pl.ds(0, bulk)], a2a_recv.at[c]).wait()
        high, low = split2(recv[c])
        both = jnp.dot(sel_dst[...], jnp.concatenate([high, low], axis=1), preferred_element_type=F32)
        total = both[:, 0:128] + both[:, 128:256]
        return [total[128 * yb : 128 * (yb + 1)].reshape(CZ, CX, 128) for yb in range(CY // 128)]

    for copy in loads[4:]:
        copy.wait()
    for yb, more in enumerate(incoming(0)):
        at = pl.ds(128 * yb, 128)
        kmass[:, :, at] = kmass[:, :, at] + more

    spd_copies = []
    for c in range(3):
        for yb, more in enumerate(incoming(c + 1)):
            at = pl.ds(128 * yb, 128)
            spd[c, 1 : 1 + CZ, :, at] = (kmom[c, :, :, at] + more) / kmass[:, :, at]
        plane[c, 0:8, :] = spd[c, 1 : 1 + CZ, 0, :]
        plane[c, 8:16, :] = spd[c, 1 : 1 + CZ, 1, :]
        plane[c, 16:24, :] = spd[c, 1 : 1 + CZ, CX - 1, :]
        first_x, second_x, last_x = (plane.at[c, pl.ds(8 * i, 8), :] for i in range(3))
        moves = [
            (spd.at[c, CZ], spd.at[c, 0], (up, t)),
            (spd.at[c, pl.ds(1, 2)], spd.at[c, pl.ds(1 + CZ, 2)], (down, t)),
            (first_x, xp16.at[c, pl.ds(8, 8), :], (b, left)),
            (second_x, xp17.at[c], (b, left)),
            (last_x, xm1.at[c, pl.ds(0, 8), :], (b, right)),
            (last_x, xm1.at[c, pl.ds(8, 8), :], (down, right)),
            (first_x, xp16.at[c, pl.ds(0, 8), :], (up, left)),
            (first_x, xp16.at[c, pl.ds(16, 8), :], (down, left)),
        ]
        for i, (src, dst, device) in enumerate(moves):
            copy = remote(src, dst, sp_send.at[c, i], sp_recv.at[c, i], device)
            copy.start()
            spd_copies.append(copy)
    for copy in spd_copies:
        copy.wait()

    @pl.when(at_bottom)
    def _():
        for c in range(3):
            spd[c, 0] = jnp.zeros((CX, CY), F32)
            xp16[c, 0:8, :] = nothing

    @pl.when(at_top)
    def _():
        for c in range(3):
            spd[c, 1 + CZ : 3 + CZ] = jnp.zeros((2, CX, CY), F32)
            xm1[c, 8:16, :] = nothing
            xp16[c, 16:24, :] = nothing

    @pl.when(at_left)
    def _():
        for c in range(3):
            xm1[c] = jnp.zeros((16, CY), F32)

    @pl.when(at_right)
    def _():
        for c in range(3):
            xp16[c] = jnp.zeros((24, CY), F32)
            xp17[c] = nothing

    def squared(here, *others):
        total = jnp.zeros_like(here)
        for other in others:
            change = other - here
            total = total + change * change
        return total

    squares_m = jnp.zeros((CZ, CY), F32)
    squares_p = jnp.zeros((CZ, CY), F32)
    for c in range(3):
        whole = xm1[c]
        here = whole[0:8]
        above = pltpu.roll(whole, 15, 0)[0:8]
        squares_m = squares_m + squared(here, above, plane[c, 0:8, :], ahead_y(here))
        whole = xp16[c]
        here = whole[8:16]
        above = pltpu.roll(whole, 23, 0)[8:16]
        squares_p = squares_p + squared(here, above, xp17[c], ahead_y(here))
    visc_m = jnp.where(at_left, 0.0, visc_of(squares_m))
    visc_p = jnp.where(at_right, 0.0, visc_of(squares_p))
    plane[0, 0:8, :] = visc_m
    plane[0, 8:16, :] = visc_p
    here = xp16[0]
    div = here[8:16] - pltpu.roll(here, 1, 0)[8:16]
    div = div + (xp16[1, 8:16, :] - plane[1, 16:24, :])
    here = xp16[2, 8:16, :]
    div = div + (here - behind_y(here))
    plane[0, 16:24, :] = jnp.where(at_right, 0.0, -penalty_factor * div)

    def viscosity(i, carry):
        squares = jnp.zeros((CX, CY), F32)
        for c in range(3):
            here = spd[c, i]
            edge = xp16[c, pl.ds(i + 7, 1), :]
            squares = squares + squared(here, spd[c, i + 1], ahead_x(here, edge), ahead_y(here))
        z = i - 1
        inside = ((z >= 0) | jnp.logical_not(at_bottom)) & ((z < CZ) | jnp.logical_not(at_top))
        visc[i] = jnp.where(inside, visc_of(squares), 0.0)
        return carry

    lax.fori_loop(0, CZ + 2, viscosity, 0)

    def pressure(z, carry):
        here = spd[0, z + 1]
        div = here - spd[0, z]
        here = spd[1, z + 1]
        div = div + (here - behind_x(here, xm1[1, pl.ds(z, 1), :]))
        here = spd[2, z + 1]
        div = div + (here - behind_y(here))
        inside = (z < CZ) | jnp.logical_not(at_top)
        pres[z] = jnp.where(inside, -penalty_factor * div, 0.0)
        return carry

    lax.fori_loop(0, CZ + 1, pressure, 0)

    def update(z, carry):
        v = visc[z + 1]
        line = pl.ds(z, 1)
        v_next = (visc[z + 2], ahead_x(v, plane[0, pl.ds(z + 8, 1), :]), ahead_y(v))
        v_prev = (visc[z], behind_x(v, plane[0, line, :]), behind_y(v))
        forward = [0.5 * (v + other) for other in v_next]
        backward = [0.5 * (v + other) for other in v_prev]
        density = kmass[z] / vol[z]
        bottom = forward[0] + backward[0] + forward[1] + backward[1] + forward[2] + backward[2] + density
        p = pres[z]
        p_next = (pres[z + 1], ahead_x(p, plane[0, pl.ds(z + 16, 1), :]), ahead_y(p))
        for c in range(3):
            here = spd[c, z + 1]
            top = forward[0] * spd[c, z + 2] + backward[0] * spd[c, z]
            top = top + forward[1] * ahead_x(here, xp16[c, pl.ds(z + 8, 1), :])
            top = top + backward[1] * behind_x(here, xm1[c, line, :])
            top = top + forward[2] * ahead_y(here) + backward[2] * behind_y(here)
            top = top - (p_next[c] - p) + trac[c] + density * here
            vel_ref[c, z] = top / bottom
        return carry

    lax.fori_loop(0, CZ, update, 0)

    for c in range(COMPS):
        pltpu.make_async_copy(send.at[c, pl.ds(0, bulk)], send.at[c, pl.ds(0, bulk)], a2a_send.at[c]).wait()
    pltpu.make_async_copy(ids_send.at[pl.ds(1, N_TILE - 1)], ids_send.at[pl.ds(1, N_TILE - 1)], ids_ssem).wait()
    regrid_out.wait()


def shards(
    displacement, old_mass, old_momentum, intersection_fraction, entry_order, target_owner,
    target_block, kept_mass, kept_momentum, surface_panels, panel_ids, contact_flags,
):
    grid = jax.ShapeDtypeStruct((3, CZ, CX, CY), F32)
    hbm, vmem = pl.BlockSpec(memory_space=pl.ANY), pl.BlockSpec(memory_space=pltpu.VMEM)
    dma = pltpu.SemaphoreType.DMA
    return pl.pallas_call(
        kernel,
        out_shape=(grid, grid),
        in_specs=[hbm, hbm, hbm, hbm, vmem, vmem, vmem, hbm, hbm, vmem, vmem, vmem],
        out_specs=(hbm, vmem),
        scratch_shapes=[
            pltpu.VMEM((3, CZ + 6, 32, CY), F32),
            pltpu.VMEM((3, CZ + 6, 32, CY), F32),
            pltpu.VMEM((COMPS, NBLK, 128), F32),
            pltpu.VMEM((NBLK, 128), F32),
            pltpu.VMEM((CZ, CX, CY), F32),
            pltpu.VMEM((3, CZ, CX, CY), F32),
            pltpu.VMEM((CZ, CX, CY), F32),
            pltpu.VMEM((GROUPS, ROWS, OV), BF16),
            pltpu.VMEM((2 * NBLK, 256), BF16),
            pltpu.VMEM((COMPS, N_TILE * CAP, 128), F32),
            pltpu.VMEM((COMPS, RROWS, 128), F32),
            pltpu.VMEM((N_TILE, 1, 128), F32),
            pltpu.VMEM((N_TILE, 1, 128), F32),
            pltpu.VMEM((NBLK, RROWS), BF16),
            pltpu.VMEM((2, 72, CY), F32),
            pltpu.VMEM((72, CY), F32),
            pltpu.VMEM((72, CY), F32),
            pltpu.VMEM((4, 16, CY), F32),
            pltpu.VMEM((4, 16, CY), F32),
            pltpu.VMEM((N_TILE, 3, 4, 128), F32),
            pltpu.VMEM((3, CX, CY), F32),
            pltpu.VMEM((3, CZ + 3, CX, CY), F32),
            pltpu.VMEM((3, 24, CY), F32),
            pltpu.VMEM((3, 16, CY), F32),
            pltpu.VMEM((3, 24, CY), F32),
            pltpu.VMEM((3, 8, CY), F32),
            pltpu.VMEM((CZ + 2, CX, CY), F32),
            pltpu.VMEM((CZ + 1, CX, CY), F32),
            dma((6,)),
            dma((1,)),
            dma((COMPS,)),
            dma((COMPS,)),
            dma,
            dma,
            dma((8,)),
            dma((8,)),
            dma((TY - 1,)),
            dma((TY - 1,)),
            dma((TX - 1,)),
            dma((TX - 1,)),
            dma((3, 8)),
            dma((3, 8)),
        ],
        compiler_params=pltpu.CompilerParams(
            collective_id=0, has_side_effects=True, vmem_limit_bytes=48 * 2**20
        ),
    )(
        displacement,
        old_mass,
        old_momentum.transpose(1, 0, 2),
        intersection_fraction,
        entry_order,
        target_owner.reshape(1, OV),
        target_block.reshape(1, OV),
        kept_mass,
        kept_momentum,
        surface_panels.transpose(1, 0, 2),
        panel_ids[0].T,
        contact_flags[0].T,
    )


def solution(mesh):
    return jax.shard_map(
        shards,
        mesh=mesh,
        in_specs=(
            P(None, "band", "tile", None),
            P(("band", "tile"), None),
            P(("band", "tile"), None, None),
            P(("band", "tile"), None),
            P(("band", "tile"), None),
            P(("band", "tile"), None),
            P(("band", "tile")),
            P("band", "tile", None),
            P(None, "band", "tile", None),
            P(("band", "tile"), None, None),
            P("band", "tile", None),
            P("band", "tile", None),
        ),
        out_specs=(P(None, "band", "tile", None), P(None, "band", "tile", None)),
        check_vma=False,
    )
```

```python
import jax
import jax.numpy as jnp
from jax import lax
from jax.experimental import pallas as pl
from jax.experimental.pallas import tpu as pltpu
from jax.sharding import PartitionSpec as P

MESH = pl.DeviceIdType.MESH
F32, BF16 = jnp.float32, jnp.bfloat16

relax_factor = 0.8
cell_fraction = 0.1
strain_eps = 0.05
rate_power = -0.4
penalty_factor = 0.5

N_BAND, N_TILE = 16, 32
TX, TY = 4, 8
CZ, CX, CY = 8, 16, 512
OV, NBLK, CAP = 1024, 512, 40
COMPS = 4
GROUP = 4
GROUPS = N_TILE // GROUP
ROWS = GROUP * CAP
SETS = (N_TILE + 2) // 3
RROWS = SETS * 128
TOP = 8
PLANES = ((0, 1), (0, 2), (1, 1), (1, 2), (1, 3), (2, 1), (2, 2))
LINES = ((0, 1, 1), (0, 1, 2), (0, 2, 1), (1, 1, 1), (1, 1, 2), (1, 2, 1), (2, 1, 1))
PARTS = ((0, 4), (4, 8), (8, SETS))


def slot_row(k):
    return 128 * (k // 3) + CAP * (k % 3)


def split2(value):
    high = value.astype(BF16)
    low = (value - high.astype(F32)).astype(BF16)
    return high, low


def iota(shape, dim):
    return lax.broadcasted_iota(jnp.int32, shape, dim)


def ahead_y(f):
    n = f.shape[-1]
    return jnp.where(iota(f.shape, f.ndim - 1) == n - 1, 0.0, pltpu.roll(f, n - 1, f.ndim - 1))


def behind_y(f):
    return jnp.where(iota(f.shape, f.ndim - 1) == 0, 0.0, pltpu.roll(f, 1, f.ndim - 1))


def ahead_x(f, row):
    n = f.shape[0]
    return jnp.where(iota(f.shape, 0) == n - 1, row, pltpu.roll(f, n - 1, 0))


def behind_x(f, row):
    return jnp.where(iota(f.shape, 0) == 0, row, pltpu.roll(f, 1, 0))


def visc_of(squares):
    return jnp.exp(rate_power * jnp.log(strain_eps + squares))


def kernel(
    disp_hbm, mass_hbm, mom_hbm, frac_hbm, order_hbm, owner_hbm, block_hbm,
    kmass_hbm, kmom_hbm, panels_hbm, pids_hbm, flags_hbm,
    regrid_ref, vel_ref,
    order_ref, owner_ref, block_ref, panels_ref, pids_ref, flags_ref,
    ext, s1, old, frac, kmass, kmom, vol, sel_src, table, send, recv, ids_send, ids_recv,
    sel_dst, xst, xhl, xhr, cst, chl, pans, trac, spd, plane, xm1, xp16, qst, xq, crs, crn, side, visc, pres,
    small_sem, load_sem, out_sem, a2a_send, a2a_recv, ids_ssem, ids_rsem, dh_send, dh_recv,
    py_send, py_recv, px_send, px_recv, sp_send, sp_recv,
):
    b = lax.axis_index("band")
    t = lax.axis_index("tile")
    tx, ty = t // TY, t % TY
    up, down = (b + 1) % N_BAND, (b + N_BAND - 1) % N_BAND
    right, left = (t + 1) % N_TILE, (t + N_TILE - 1) % N_TILE

    def peer(k):
        return ((tx + k // TY) % TX) * TY + (ty + k % TY) % TY

    barrier = pltpu.get_barrier_semaphore()
    partners = [(b, peer(k)) for k in range(1, N_TILE)]
    partners += [(up, t), (down, t), (up, right), (up, left), (down, right), (down, left)]
    for partner in partners:
        pl.semaphore_signal(barrier, inc=1, device_id=partner, device_id_type=MESH)

    small = [(owner_hbm, owner_ref), (order_hbm, order_ref), (block_hbm, block_ref),
             (panels_hbm, panels_ref), (pids_hbm, pids_ref), (flags_hbm, flags_ref)]
    small = [pltpu.make_async_copy(src, dst, small_sem.at[i]) for i, (src, dst) in enumerate(small)]
    loads = [
        pltpu.make_async_copy(disp_hbm, ext.at[:, pl.ds(3, CZ), pl.ds(TOP, CX), :], load_sem.at[0]),
        pltpu.make_async_copy(frac_hbm, frac, load_sem.at[1]),
        pltpu.make_async_copy(mass_hbm, old.at[0], load_sem.at[2]),
        pltpu.make_async_copy(mom_hbm, old.at[pl.ds(1, 3)], load_sem.at[3]),
        pltpu.make_async_copy(kmass_hbm, kmass, load_sem.at[4]),
        pltpu.make_async_copy(kmom_hbm, kmom, load_sem.at[5]),
    ]
    loads[0].start()
    for copy in small + loads[1:]:
        copy.start()

    loads[0].wait()
    for i, (c, d) in enumerate(PLANES):
        at = pl.ds(8 * i, 8)
        xst[0, at, :] = ext[c, 3:11, TOP + CX - d, :]
        xst[1, at, :] = ext[c, 3:11, TOP + d - 1, :]
    for corner in range(4):
        sz, sx = corner // 2, corner % 2
        for i, (c, dz, dx) in enumerate(LINES):
            z = CZ - dz if sz else dz - 1
            x = CX - dx if sx else dx - 1
            cst[corner, i] = ext[c, 3 + z, pl.ds(TOP + x, 1), :]
    for copy in small:
        copy.wait()
    pans[ty] = panels_ref[...]

    pl.semaphore_wait(barrier, len(partners))

    def remote(src, dst, ssem, rsem, device):
        return pltpu.make_async_remote_copy(
            src_ref=src, dst_ref=dst, send_sem=ssem, recv_sem=rsem, device_id=device, device_id_type=MESH
        )

    disp_copies = [
        remote(xst.at[0], xhl, dh_send.at[0], dh_recv.at[0], (b, right)),
        remote(xst.at[1], xhr, dh_send.at[1], dh_recv.at[1], (b, left)),
        remote(disp_hbm.at[:, pl.ds(CZ - 3, 3)], ext.at[:, pl.ds(0, 3), pl.ds(TOP, CX), :],
               dh_send.at[2], dh_recv.at[2], (up, t)),
        remote(disp_hbm.at[:, pl.ds(0, 3)], ext.at[:, pl.ds(3 + CZ, 3), pl.ds(TOP, CX), :],
               dh_send.at[3], dh_recv.at[3], (down, t)),
    ]
    for corner in range(4):
        sz, sx = corner // 2, corner % 2
        disp_copies.append(
            remote(cst.at[corner], chl.at[corner], dh_send.at[4 + corner], dh_recv.at[4 + corner],
                   (up if sz else down, right if sx else left))
        )
    for copy in disp_copies:
        copy.start()
    panel_y = [
        remote(pans.at[ty], pans.at[ty], py_send.at[i - 1], py_recv.at[i - 1], (b, tx * TY + (ty + i) % TY))
        for i in range(1, TY)
    ]
    for copy in panel_y:
        copy.start()

    owner = owner_ref[...]
    column = iota((N_TILE, 1), 0)
    column_dest = ((tx + column // TY) % TX) * TY + (ty + column % TY) % TY
    before = (iota((128, 128), 0) < iota((128, 128), 1)).astype(BF16)
    base = jnp.zeros((N_TILE, 1), F32)
    slots, names = [], []
    for j in range(OV // 128):
        hot = (owner[:, 128 * j : 128 * (j + 1)] == column_dest).astype(F32)
        prefix = base + jnp.dot(hot.astype(BF16), before, preferred_element_type=F32)
        slots.append(jnp.sum(hot * prefix, axis=0, keepdims=True))
        names.append(jnp.sum(hot * column.astype(F32), axis=0, keepdims=True))
        base = base + jnp.sum(hot, axis=1, keepdims=True)
    slot = jnp.concatenate(slots, axis=1)
    name = jnp.concatenate(names, axis=1)
    place = name * CAP + slot
    order = order_ref[...]
    code = (order // 2 + (order % 2) * NBLK + 1).astype(F32)

    block = block_ref[...]
    target = (block % 4) * 128 + block // 4 + 1
    hot = owner == column_dest
    high = jnp.where(hot, target // 16, 0).astype(F32).astype(BF16)
    low = jnp.where(hot, target % 16, 0).astype(F32).astype(BF16)
    lanes = (slot == iota((128, 1), 0).astype(F32)).astype(F32).astype(BF16)
    dims = (((1,), (1,)), ((), ()))
    ids = 16.0 * lax.dot_general(high, lanes, dims, preferred_element_type=F32)
    ids = ids + lax.dot_general(low, lanes, dims, preferred_element_type=F32)
    third = iota((N_TILE, 128), 0) % 3
    ids = jnp.where(
        third == 0, ids, jnp.where(third == 1, pltpu.roll(ids, CAP, 1), pltpu.roll(ids, 2 * CAP, 1))
    )
    for k in range(N_TILE):
        ids_send[k] = ids[k : k + 1, :]
    ids_recv[0] = ids[0:1, :]

    ids_copies = [
        remote(ids_send.at[k], ids_recv.at[k], ids_ssem, ids_rsem, (b, peer(k))) for k in range(1, N_TILE)
    ]

    for copy in ids_copies:
        copy.start()

    for copy in loads[1:4]:
        copy.wait()

    def fill_table(c):
        share = frac[...]
        values = old[c]
        one = share * values
        high, low = split2(one)
        table[0:NBLK, 0:128] = high
        table[0:NBLK, 128:256] = low
        high, low = split2((1.0 - share) * values)
        table[NBLK : 2 * NBLK, 0:128] = high
        table[NBLK : 2 * NBLK, 128:256] = low

    def rows_copy(c, k):
        return remote(
            send.at[c, pl.ds(CAP * k, CAP), :], recv.at[c, pl.ds(slot_row(k), CAP), :],
            a2a_send.at[c], a2a_recv.at[c + (c // 3) * (k // 12)], (b, peer(k)),
        )

    def dispatch(c, g):
        both = jnp.dot(sel_src[g], table[...], preferred_element_type=F32)
        rows = both[:, 0:128] + both[:, 128:256]
        send[c, pl.ds(ROWS * g, ROWS), :] = rows
        if g == 0:
            recv[c, 0:CAP, :] = rows[0:CAP]
        for j in range(GROUP):
            k = GROUP * g + j
            if k:
                rows_copy(c, k).start()

    fill_table(0)
    for g in range(GROUPS):
        wanted = (ROWS * g + iota((ROWS, 1), 0)).astype(F32)
        code_of = jnp.sum(jnp.where(place == wanted, code, 0.0), axis=1, keepdims=True)
        hit = code_of.astype(jnp.int32) == iota((ROWS, OV), 1) + 1
        sel_src[g] = jnp.where(hit, 1.0, 0.0).astype(BF16)
        dispatch(0, g)

    for i, copy in enumerate(panel_y):
        copy.wait()

    panel_x = [
        remote(pans.at[pl.ds(0, TY)], pans.at[pl.ds(TY * i, TY)], px_send.at[i - 1], px_recv.at[i - 1],
               (b, ((tx + i) % TX) * TY + ty))
        for i in range(1, TX)
    ]
    for copy in panel_x:
        copy.start()

    def later(c, carry):
        fill_table(c)
        for g in range(GROUPS):
            dispatch(c, g)
        return carry

    lax.fori_loop(1, COMPS, later, 0)

    for copy in disp_copies:
        copy.wait()
    at_left, at_right = t == 0, t == N_TILE - 1
    at_bottom, at_top = b == 0, b == N_BAND - 1
    nothing = jnp.zeros((8, CY), F32)
    for i, (c, d) in enumerate(PLANES):
        at = pl.ds(8 * i, 8)
        ext[c, 3:11, TOP - d, :] = jnp.where(at_left, nothing, xhl[at, :])
        ext[c, 3:11, TOP + CX - 1 + d, :] = jnp.where(at_right, nothing, xhr[at, :])

    @pl.when(at_bottom)
    def _():
        ext[:, 0:3, TOP : TOP + CX, :] = jnp.zeros((3, 3, CX, CY), F32)

    @pl.when(at_top)
    def _():
        ext[:, 3 + CZ : 6 + CZ, TOP : TOP + CX, :] = jnp.zeros((3, 3, CX, CY), F32)

    for corner in range(4):
        sz, sx = corner // 2, corner % 2
        outside = (at_bottom if sz else at_top) | (at_left if sx else at_right)
        for i, (c, dz, dx) in enumerate(LINES):
            z = -dz if sz else CZ - 1 + dz
            x = -dx if sx else CX - 1 + dx
            line = chl[corner, i]
            ext[c, 3 + z, pl.ds(TOP + x, 1), :] = jnp.where(outside, jnp.zeros_like(line), line)

    row = iota((32, CY), 0) - TOP
    keep_x = ((row >= 0) | jnp.logical_not(at_left)) & ((row < CX) | jnp.logical_not(at_right))

    def sweep(src, dst, c, zi):
        here = src[c, zi]
        near = src[c, zi + 1] + src[c, zi - 1]
        near = near + pltpu.roll(here, 1, 0) + pltpu.roll(here, 31, 0)
        near = near + ahead_y(here) + behind_y(here)
        new = here + relax_factor * (near / 6.0 - here)
        z = zi - 3
        inside = ((z >= 0) | jnp.logical_not(at_bottom)) & ((z < CZ) | jnp.logical_not(at_top))
        dst[c, zi] = jnp.where(keep_x & inside, new, 0.0)

    def first(zi, carry):
        for c in range(3):
            sweep(ext, s1, c, zi)
        return carry

    def second(zi, carry):
        for c in range(3):
            sweep(s1, ext, c, zi)
        return carry

    lax.fori_loop(1, 13, first, 0)
    lax.fori_loop(2, 12, second, 0)
    regrid_out = pltpu.make_async_copy(
        ext.at[:, pl.ds(3, CZ), pl.ds(TOP, CX), :], regrid_ref, out_sem.at[0]
    )
    regrid_out.start()

    def volumes(z, carry):
        zi = z + 3
        own = pl.ds(TOP, CX)
        stretch = ext[0, zi + 1, own, :] - ext[0, zi - 1, own, :]
        across = ext[1, zi]
        across = pltpu.roll(across, 31, 0) - pltpu.roll(across, 1, 0)
        along = ext[2, zi, own, :]
        stretch = stretch + across[TOP : TOP + CX] + (ahead_y(along) - behind_y(along))
        vol[z] = 1.0 + cell_fraction * (0.5 * stretch)
        return carry

    lax.fori_loop(0, CZ, volumes, 0)

    for copy in panel_x:
        copy.wait()
    source = iota((N_TILE * 4, CX), 0)
    member = source // 4
    panel = ((tx + TX - member // TY) % TX) * (TY * 4) + (member % TY) * 4 + source % 4
    for yb in range(CY // 128):
        chosen = (panel == pids_ref[yb : yb + 1, :]) & (flags_ref[yb : yb + 1, :] != 0)
        chosen = jnp.where(chosen, 1.0, 0.0)
        for c in range(3):
            faces = pans[:, c].reshape(N_TILE * 4, 128)
            high, low = split2(faces)
            tn = (((0,), (0,)), ((), ()))
            weight = chosen.astype(BF16)
            got = lax.dot_general(weight, high, tn, preferred_element_type=F32)
            got = got + lax.dot_general(weight, low, tn, preferred_element_type=F32)
            trac[c, :, 128 * yb : 128 * (yb + 1)] = got

    bulk = (N_TILE - 1) * CAP
    pltpu.make_async_copy(ids_recv.at[pl.ds(1, N_TILE - 1)], ids_recv.at[pl.ds(1, N_TILE - 1)], ids_rsem).wait()
    number = iota((NBLK, 128), 0).astype(F32) + 1.0
    for s in range(SETS):
        line = ids_recv[3 * s]
        for k in range(3 * s + 1, min(3 * s + 3, N_TILE)):
            line = line + ids_recv[k]
        sel_dst[:, 128 * s : 128 * (s + 1)] = jnp.where(number == line, 1.0, 0.0).astype(BF16)
    for s in range(SETS):
        used = CAP * min(3, N_TILE - 3 * s)
        for c in range(COMPS):
            recv[c, 128 * s + used : 128 * (s + 1), :] = jnp.zeros((128 - used, 128), F32)

    def arrived(c, first, last, sem):
        rows = CAP * (min(3 * last, N_TILE) - max(3 * first, 1))
        pltpu.make_async_copy(recv.at[c, pl.ds(0, rows)], recv.at[c, pl.ds(0, rows)], sem).wait()
        at = pl.ds(128 * first, 128 * (last - first))
        high, low = split2(recv[c, at, :])
        both = jnp.dot(sel_dst[:, at], jnp.concatenate([high, low], axis=1), preferred_element_type=F32)
        return both[:, 0:128] + both[:, 128:256]

    def incoming(c):
        if c < 3:
            total = arrived(c, 0, SETS, a2a_recv.at[c])
        else:
            total = sum(arrived(c, *part, a2a_recv.at[c + i]) for i, part in enumerate(PARTS))
        return [total[128 * yb : 128 * (yb + 1)].reshape(CZ, CX, 128) for yb in range(CY // 128)]

    for copy in loads[4:]:
        copy.wait()
    for yb, more in enumerate(incoming(0)):
        at = pl.ds(128 * yb, 128)
        kmass[:, :, at] = kmass[:, :, at] + more

    spd_copies = []

    def send_speed(moves):
        for src, dst, device in moves:
            i = len(spd_copies)
            spd_copies.append(remote(src, dst, sp_send.at[i], sp_recv.at[i], device))
            spd_copies[-1].start()

    across = jnp.zeros((CZ, CY), F32)
    for c in range(3):
        for yb, more in enumerate(incoming(c + 1)):
            at = pl.ds(128 * yb, 128)
            spd[c, 1 : 1 + CZ, :, at] = (kmom[c, :, :, at] + more) / kmass[:, :, at]
        first_x = spd[c, 1 : 1 + CZ, 0, :]
        last_x = spd[c, 1 : 1 + CZ, CX - 1, :]
        plane[c, 0:8, :] = first_x
        plane[c, 8:16, :] = last_x
        send_speed((
            (plane.at[c, pl.ds(0, 8), :], xp16.at[c, pl.ds(8, 8), :], (b, left)),
            (plane.at[c, pl.ds(8, 8), :], xm1.at[c, pl.ds(0, 8), :], (b, right)),
            (spd.at[c, CZ], spd.at[c, 0], (up, t)),
            (spd.at[c, pl.ds(1, 2)], spd.at[c, pl.ds(1 + CZ, 2)], (down, t)),
        ))
        change = spd[c, 1 : 1 + CZ, 1, :] - first_x
        across = across + change * change
        crs[0, c] = last_x[0:1]
        crs[1, c] = first_x[7:8]
        crs[2, c] = first_x[0:1]
    qst[...] = across
    send_speed((
        (qst, xq, (b, left)),
        (crs.at[0], crn.at[0], (down, right)),
        (crs.at[1], crn.at[1], (up, left)),
        (crs.at[2], crn.at[2], (down, left)),
    ))

    def squared(here, *others):
        total = jnp.zeros_like(here)
        for other in others:
            change = other - here
            total = total + change * change
        return total

    def viscosity(i, edge):
        squares = jnp.zeros((CX, CY), F32)
        for c in range(3):
            here = spd[c, i]
            row = here if edge is None else xp16[c, edge : edge + 1, :]
            squares = squares + squared(here, spd[c, i + 1], ahead_x(here, row), ahead_y(here))
        visc[i] = visc_of(squares)

    def pressure(z, edge):
        here = spd[0, z + 1]
        div = here - spd[0, z]
        here = spd[1, z + 1]
        div = div + (here - behind_x(here, here if edge is None else xm1[1, edge : edge + 1, :]))
        here = spd[2, z + 1]
        div = div + (here - behind_y(here))
        pres[z] = -penalty_factor * div

    lax.fori_loop(1, CZ, lambda i, carry: (viscosity(i, None), carry)[1], 0)
    lax.fori_loop(1, CZ, lambda z, carry: (pressure(z, None), carry)[1], 0)

    for copy in spd_copies:
        copy.wait()
    for c in range(3):
        xm1[c, 8:9, :] = crn[0, c]
        xp16[c, 7:8, :] = crn[1, c]
        xp16[c, 16:17, :] = crn[2, c]

    @pl.when(at_bottom)
    def _():
        for c in range(3):
            spd[c, 0] = jnp.zeros((CX, CY), F32)
            xp16[c, 0:8, :] = nothing

    @pl.when(at_top)
    def _():
        for c in range(3):
            spd[c, 1 + CZ : 3 + CZ] = jnp.zeros((2, CX, CY), F32)
            xm1[c, 8:16, :] = nothing
            xp16[c, 16:24, :] = nothing

    @pl.when(at_left)
    def _():
        for c in range(3):
            xm1[c] = jnp.zeros((16, CY), F32)

    @pl.when(at_right)
    def _():
        for c in range(3):
            xp16[c] = jnp.zeros((24, CY), F32)

    squares_m = jnp.zeros((CZ, CY), F32)
    squares_l = jnp.zeros((CZ, CY), F32)
    squares_p = xq[...]
    for c in range(3):
        whole = xm1[c]
        here = whole[0:8]
        above = pltpu.roll(whole, 15, 0)[0:8]
        squares_m = squares_m + squared(here, above, plane[c, 0:8, :], ahead_y(here))
        whole = xp16[c]
        here = whole[8:16]
        above = pltpu.roll(whole, 23, 0)[8:16]
        squares_p = squares_p + squared(here, above, ahead_y(here))
        last = plane[c, 8:16, :]
        above = ahead_x(last, spd[c, 1 + CZ, CX - 1 : CX, :])
        squares_l = squares_l + squared(last, above, here, ahead_y(last))
    side[0:8, :] = jnp.where(at_left, 0.0, visc_of(squares_m))
    side[8:16, :] = jnp.where(at_right, 0.0, visc_of(squares_p))
    here = xp16[0]
    div = here[8:16] - pltpu.roll(here, 1, 0)[8:16]
    div = div + (xp16[1, 8:16, :] - plane[1, 8:16, :])
    here = xp16[2, 8:16, :]
    div = div + (here - behind_y(here))
    side[16:24, :] = jnp.where(at_right, 0.0, -penalty_factor * div)
    here = plane[0, 0:8, :]
    div = here - behind_x(here, spd[0, 0, 0:1, :])
    div = div + (plane[1, 0:8, :] - xm1[1, 0:8, :])
    here = plane[2, 0:8, :]
    div = div + (here - behind_y(here))

    viscosity(0, 7)
    viscosity(CZ, 15)
    viscosity(CZ + 1, 16)
    pressure(0, 0)
    pressure(CZ, 8)
    visc[1 : 1 + CZ, CX - 1, :] = visc_of(squares_l)
    pres[0:CZ, 0, :] = -penalty_factor * div

    @pl.when(at_bottom)
    def _():
        visc[0] = jnp.zeros((CX, CY), F32)

    @pl.when(at_top)
    def _():
        visc[CZ + 1] = jnp.zeros((CX, CY), F32)
        pres[CZ] = jnp.zeros((CX, CY), F32)

    def update(z, carry):
        v = visc[z + 1]
        line = pl.ds(z, 1)
        v_next = (visc[z + 2], ahead_x(v, side[pl.ds(z + 8, 1), :]), ahead_y(v))
        v_prev = (visc[z], behind_x(v, side[line, :]), behind_y(v))
        forward = [0.5 * (v + other) for other in v_next]
        backward = [0.5 * (v + other) for other in v_prev]
        density = kmass[z] / vol[z]
        bottom = forward[0] + backward[0] + forward[1] + backward[1] + forward[2] + backward[2] + density
        p = pres[z]
        p_next = (pres[z + 1], ahead_x(p, side[pl.ds(z + 16, 1), :]), ahead_y(p))
        for c in range(3):
            here = spd[c, z + 1]
            top = forward[0] * spd[c, z + 2] + backward[0] * spd[c, z]
            top = top + forward[1] * ahead_x(here, xp16[c, pl.ds(z + 8, 1), :])
            top = top + backward[1] * behind_x(here, xm1[c, line, :])
            top = top + forward[2] * ahead_y(here) + backward[2] * behind_y(here)
            top = top - (p_next[c] - p) + trac[c] + density * here
            vel_ref[c, z] = top / bottom
        return carry

    lax.fori_loop(0, CZ, update, 0)

    for c in range(COMPS):
        pltpu.make_async_copy(send.at[c, pl.ds(0, bulk)], send.at[c, pl.ds(0, bulk)], a2a_send.at[c]).wait()
    pltpu.make_async_copy(ids_send.at[pl.ds(1, N_TILE - 1)], ids_send.at[pl.ds(1, N_TILE - 1)], ids_ssem).wait()
    regrid_out.wait()


def store(regrid_ref, vel_ref, regrid_hbm, vel_hbm, sem):
    copies = [
        pltpu.make_async_copy(regrid_ref, regrid_hbm, sem.at[0]),
        pltpu.make_async_copy(vel_ref, vel_hbm, sem.at[1]),
    ]
    for copy in copies:
        copy.start()
    for copy in copies:
        copy.wait()


def shards(
    displacement, old_mass, old_momentum, intersection_fraction, entry_order, target_owner,
    target_block, kept_mass, kept_momentum, surface_panels, panel_ids, contact_flags,
):
    grid = jax.ShapeDtypeStruct((3, CZ, CX, CY), F32)
    hbm, vmem = pl.BlockSpec(memory_space=pltpu.HBM), pl.BlockSpec(memory_space=pltpu.VMEM)
    dma = pltpu.SemaphoreType.DMA
    regridded, velocity = pl.pallas_call(
        kernel,
        out_shape=(pltpu.VMEM(grid.shape, F32), pltpu.VMEM(grid.shape, F32)),
        in_specs=[hbm] * 12,
        out_specs=(vmem, vmem),
        scratch_shapes=[
            pltpu.VMEM((1, OV), jnp.int32),
            pltpu.VMEM((1, OV), jnp.int32),
            pltpu.VMEM((1, OV), jnp.int32),
            pltpu.VMEM((3, 4, 128), F32),
            pltpu.VMEM((4, CX), jnp.int32),
            pltpu.VMEM((4, CX), jnp.int32),
            pltpu.VMEM((3, CZ + 6, 32, CY), F32),
            pltpu.VMEM((3, CZ + 6, 32, CY), F32),
            pltpu.VMEM((COMPS, NBLK, 128), F32),
            pltpu.VMEM((NBLK, 128), F32),
            pltpu.VMEM((CZ, CX, CY), F32),
            pltpu.VMEM((3, CZ, CX, CY), F32),
            pltpu.VMEM((CZ, CX, CY), F32),
            pltpu.VMEM((GROUPS, ROWS, OV), BF16),
            pltpu.VMEM((2 * NBLK, 256), BF16),
            pltpu.VMEM((COMPS, N_TILE * CAP, 128), F32),
            pltpu.VMEM((COMPS, RROWS, 128), F32),
            pltpu.VMEM((N_TILE, 1, 128), F32),
            pltpu.VMEM((N_TILE, 1, 128), F32),
            pltpu.VMEM((NBLK, RROWS), BF16),
            pltpu.VMEM((2, 8 * len(PLANES), CY), F32),
            pltpu.VMEM((8 * len(PLANES), CY), F32),
            pltpu.VMEM((8 * len(PLANES), CY), F32),
            pltpu.VMEM((4, len(LINES), 1, CY), F32),
            pltpu.VMEM((4, len(LINES), 1, CY), F32),
            pltpu.VMEM((N_TILE, 3, 4, 128), F32),
            pltpu.VMEM((3, CX, CY), F32),
            pltpu.VMEM((3, CZ + 3, CX, CY), F32),
            pltpu.VMEM((3, 16, CY), F32),
            pltpu.VMEM((3, 16, CY), F32),
            pltpu.VMEM((3, 24, CY), F32),
            pltpu.VMEM((8, CY), F32),
            pltpu.VMEM((8, CY), F32),
            pltpu.VMEM((3, 3, 1, CY), F32),
            pltpu.VMEM((3, 3, 1, CY), F32),
            pltpu.VMEM((24, CY), F32),
            pltpu.VMEM((CZ + 2, CX, CY), F32),
            pltpu.VMEM((CZ + 1, CX, CY), F32),
            dma((6,)),
            dma((6,)),
            dma((1,)),
            dma((COMPS,)),
            dma((COMPS - 1 + len(PARTS),)),
            dma,
            dma,
            dma((8,)),
            dma((8,)),
            dma((TY - 1,)),
            dma((TY - 1,)),
            dma((TX - 1,)),
            dma((TX - 1,)),
            dma((16,)),
            dma((16,)),
        ],
        compiler_params=pltpu.CompilerParams(
            collective_id=0, has_side_effects=True, vmem_limit_bytes=48 * 2**20
        ),
    )(
        *(
            pltpu.with_memory_space_constraint(value, pltpu.HBM)
            for value in (
                displacement,
                old_mass,
                old_momentum.transpose(1, 0, 2),
                intersection_fraction,
                entry_order,
                target_owner.reshape(1, OV),
                target_block.reshape(1, OV),
                kept_mass,
                kept_momentum,
                surface_panels.transpose(1, 0, 2),
                panel_ids[0].T,
                contact_flags[0].T,
            )
        )
    )
    return pl.pallas_call(
        store,
        out_shape=(grid, grid),
        in_specs=[vmem, vmem],
        out_specs=(hbm, hbm),
        scratch_shapes=[dma((2,))],
        compiler_params=pltpu.CompilerParams(vmem_limit_bytes=2**20),
    )(*(pltpu.with_memory_space_constraint(value, pltpu.VMEM) for value in (regridded, velocity)))


def solution(mesh):
    return jax.shard_map(
        shards,
        mesh=mesh,
        in_specs=(
            P(None, "band", "tile", None),
            P(("band", "tile"), None),
            P(("band", "tile"), None, None),
            P(("band", "tile"), None),
            P(("band", "tile"), None),
            P(("band", "tile"), None),
            P(("band", "tile")),
            P("band", "tile", None),
            P(None, "band", "tile", None),
            P(("band", "tile"), None, None),
            P("band", "tile", None),
            P("band", "tile", None),
        ),
        out_specs=(P(None, "band", "tile", None), P(None, "band", "tile", None)),
        check_vma=False,
    )
```

```python
import jax
import jax.numpy as jnp
from jax import lax
from jax.experimental import pallas as pl
from jax.experimental.pallas import tpu as pltpu
from jax.sharding import PartitionSpec as P

MESH = pl.DeviceIdType.MESH
F32, BF16 = jnp.float32, jnp.bfloat16

relax_factor = 0.8
cell_fraction = 0.1
strain_eps = 0.05
rate_power = -0.4
penalty_factor = 0.5

N_BAND, N_TILE = 16, 32
TX, TY = 4, 8
CZ, CX, CY = 8, 16, 512
OV, NBLK, CAP = 1024, 512, 40
COMPS = 4
GROUP = 4
GROUPS = N_TILE // GROUP
ROWS = GROUP * CAP
SETS = (N_TILE + 2) // 3
RROWS = SETS * 128
TOP = 8
PLANES = ((0, 1), (0, 2), (1, 1), (1, 2), (1, 3), (2, 1), (2, 2))
LINES = ((0, 1, 1), (0, 1, 2), (0, 2, 1), (1, 1, 1), (1, 1, 2), (1, 2, 1), (2, 1, 1))
PARTS = ((0, 4), (4, 8), (8, SETS))


def slot_row(k):
    return 128 * (k // 3) + CAP * (k % 3)


def split2(value):
    high = value.astype(BF16)
    low = (value - high.astype(F32)).astype(BF16)
    return high, low


def iota(shape, dim):
    return lax.broadcasted_iota(jnp.int32, shape, dim)


def ahead_y(f):
    n = f.shape[-1]
    return jnp.where(iota(f.shape, f.ndim - 1) == n - 1, 0.0, pltpu.roll(f, n - 1, f.ndim - 1))


def behind_y(f):
    return jnp.where(iota(f.shape, f.ndim - 1) == 0, 0.0, pltpu.roll(f, 1, f.ndim - 1))


def ahead_x(f, row):
    n = f.shape[0]
    return jnp.where(iota(f.shape, 0) == n - 1, row, pltpu.roll(f, n - 1, 0))


def behind_x(f, row):
    return jnp.where(iota(f.shape, 0) == 0, row, pltpu.roll(f, 1, 0))


def visc_of(squares):
    return jnp.exp(rate_power * jnp.log(strain_eps + squares))


def kernel(
    disp_hbm, mass_hbm, mom_hbm, frac_hbm, order_hbm, owner_hbm, block_hbm,
    kmass_hbm, kmom_hbm, panels_hbm, pids_hbm, flags_hbm,
    regrid_ref, vel_ref,
    order_ref, owner_ref, block_ref, panels_ref, pids_ref, flags_ref,
    ext, s1, old, frac, kmass, kmom, vol, sel_src, table, send, mid, recv, ids_send, ids_mid, ids_recv,
    sel_dst, xst, xhl, xhr, cst, chl, pans, trac, spd, plane, xm1, xp16, qst, xq, crs, crn, side, visc, pres,
    small_sem, load_sem, out_sem, a2a_send, a2a_recv, mid_recv, fwd_send, ids_ssem, ids_rsem, im_send, im_recv, dh_send, dh_recv,
    py_send, py_recv, px_send, px_recv, sp_send, sp_recv,
):
    b = lax.axis_index("band")
    t = lax.axis_index("tile")
    tx, ty = t // TY, t % TY
    up, down = (b + 1) % N_BAND, (b + N_BAND - 1) % N_BAND
    right, left = (t + 1) % N_TILE, (t + N_TILE - 1) % N_TILE

    def peer(k):
        return ((tx + k // TY) % TX) * TY + (ty + k % TY) % TY

    barrier = pltpu.get_barrier_semaphore()
    partners = [(b, peer(j)) for j in range(1, TY)] + [(b, peer(TY * i)) for i in range(1, TX)]
    for partner in partners:
        pl.semaphore_signal(barrier, inc=1, device_id=partner, device_id_type=MESH)
    at_left, at_right = t == 0, t == N_TILE - 1
    at_bottom, at_top = b == 0, b == N_BAND - 1

    def there(dz, dx):
        z_end = at_top if dz > 0 else at_bottom if dz < 0 else False
        x_end = at_right if dx > 0 else at_left if dx < 0 else False
        return jnp.logical_not(jnp.logical_or(z_end, x_end))

    def neighbour(dz, dx):
        return (up if dz > 0 else down if dz < 0 else b, right if dx > 0 else left if dx < 0 else t)

    around = [(dz, dx) for dz in (-1, 0, 1) for dx in (-1, 0, 1) if (dz, dx) != (0, 0)]
    greeted = len(partners)
    for way in around:

        @pl.when(there(*way))
        def _():
            pl.semaphore_signal(barrier, inc=1, device_id=neighbour(*way), device_id_type=MESH)

        greeted = greeted + there(*way).astype(jnp.int32)

    small = [(owner_hbm, owner_ref), (order_hbm, order_ref), (block_hbm, block_ref),
             (panels_hbm, panels_ref), (pids_hbm, pids_ref), (flags_hbm, flags_ref)]
    small = [pltpu.make_async_copy(src, dst, small_sem.at[i]) for i, (src, dst) in enumerate(small)]
    loads = [
        pltpu.make_async_copy(disp_hbm, ext.at[:, pl.ds(3, CZ), pl.ds(TOP, CX), :], load_sem.at[0]),
        pltpu.make_async_copy(frac_hbm, frac, load_sem.at[1]),
        pltpu.make_async_copy(mass_hbm, old.at[0], load_sem.at[2]),
        pltpu.make_async_copy(mom_hbm, old.at[pl.ds(1, 3)], load_sem.at[3]),
        pltpu.make_async_copy(kmass_hbm, kmass, load_sem.at[4]),
        pltpu.make_async_copy(kmom_hbm, kmom, load_sem.at[5]),
    ]
    loads[0].start()
    for copy in small + loads[1:]:
        copy.start()

    loads[0].wait()
    for i, (c, d) in enumerate(PLANES):
        at = pl.ds(8 * i, 8)
        xst[0, at, :] = ext[c, 3:11, TOP + CX - d, :]
        xst[1, at, :] = ext[c, 3:11, TOP + d - 1, :]
    for corner in range(4):
        sz, sx = corner // 2, corner % 2
        for i, (c, dz, dx) in enumerate(LINES):
            z = CZ - dz if sz else dz - 1
            x = CX - dx if sx else dx - 1
            cst[corner, i] = ext[c, 3 + z, pl.ds(TOP + x, 1), :]
    for copy in small:
        copy.wait()
    pans[ty] = panels_ref[...]

    owner = owner_ref[...]
    column = iota((N_TILE, 1), 0)
    column_dest = ((tx + column // TY) % TX) * TY + (ty + column % TY) % TY
    before = (iota((128, 128), 0) < iota((128, 128), 1)).astype(BF16)
    base = jnp.zeros((N_TILE, 1), F32)
    slots, names = [], []
    for j in range(OV // 128):
        hot = (owner[:, 128 * j : 128 * (j + 1)] == column_dest).astype(F32)
        prefix = base + jnp.dot(hot.astype(BF16), before, preferred_element_type=F32)
        slots.append(jnp.sum(hot * prefix, axis=0, keepdims=True))
        names.append(jnp.sum(hot * column.astype(F32), axis=0, keepdims=True))
        base = base + jnp.sum(hot, axis=1, keepdims=True)
    slot = jnp.concatenate(slots, axis=1)
    name = jnp.concatenate(names, axis=1)
    place = name * CAP + slot
    order = order_ref[...]
    code = (order // 2 + (order % 2) * NBLK + 1).astype(F32)

    block = block_ref[...]
    target = (block % 4) * 128 + block // 4 + 1
    hot = owner == column_dest
    high = jnp.where(hot, target // 16, 0).astype(F32).astype(BF16)
    low = jnp.where(hot, target % 16, 0).astype(F32).astype(BF16)
    lanes = (slot == iota((128, 1), 0).astype(F32)).astype(F32).astype(BF16)
    dims = (((1,), (1,)), ((), ()))
    ids = 16.0 * lax.dot_general(high, lanes, dims, preferred_element_type=F32)
    ids = ids + lax.dot_general(low, lanes, dims, preferred_element_type=F32)
    third = iota((N_TILE, 128), 0) % 3
    ids = jnp.where(
        third == 0, ids, jnp.where(third == 1, pltpu.roll(ids, CAP, 1), pltpu.roll(ids, 2 * CAP, 1))
    )
    for k in range(N_TILE):
        ids_send[k] = ids[k : k + 1, :]
    ids_recv[0] = ids[0:1, :]


    pl.semaphore_wait(barrier, greeted)

    def remote(src, dst, ssem, rsem, device):
        return pltpu.make_async_remote_copy(
            src_ref=src, dst_ref=dst, send_sem=ssem, recv_sem=rsem, device_id=device, device_id_type=MESH
        )

    class Shift:
        def __init__(self, src, dst, ssem, rsem, dz, dx):
            self.copy = remote(src, dst, ssem, rsem, neighbour(dz, dx))
            self.goes, self.comes = there(dz, dx), there(-dz, -dx)

        def start(self):
            pl.when(self.goes)(self.copy.start)

        def wait(self):
            pl.when(self.goes)(self.copy.wait_send)
            pl.when(self.comes)(self.copy.wait_recv)

    disp_copies = [
        Shift(xst.at[0], xhl, dh_send.at[0], dh_recv.at[0], 0, 1),
        Shift(xst.at[1], xhr, dh_send.at[1], dh_recv.at[1], 0, -1),
        Shift(disp_hbm.at[:, pl.ds(CZ - 3, 3)], ext.at[:, pl.ds(0, 3), pl.ds(TOP, CX), :],
              dh_send.at[2], dh_recv.at[2], 1, 0),
        Shift(disp_hbm.at[:, pl.ds(0, 3)], ext.at[:, pl.ds(3 + CZ, 3), pl.ds(TOP, CX), :],
              dh_send.at[3], dh_recv.at[3], -1, 0),
    ]
    for corner in range(4):
        sz, sx = corner // 2, corner % 2
        disp_copies.append(
            Shift(cst.at[corner], chl.at[corner], dh_send.at[4 + corner], dh_recv.at[4 + corner],
                  1 if sz else -1, 1 if sx else -1)
        )
    for copy in disp_copies:
        copy.start()
    panel_y = [
        remote(pans.at[ty], pans.at[ty], py_send.at[i - 1], py_recv.at[i - 1], (b, tx * TY + (ty + i) % TY))
        for i in range(1, TY)
    ]
    for copy in panel_y:
        copy.start()

    def column(j):
        return (b, peer(j))

    def across(i):
        return (b, peer(TY * i))

    ids_copies = [remote(ids_send.at[j], ids_recv.at[j], ids_ssem, ids_rsem, column(j)) for j in range(1, TY)]
    for i in range(1, TX):
        ids_copies += [
            remote(ids_send.at[TY * i], ids_recv.at[TY * i], ids_ssem, ids_rsem, across(i)),
            remote(ids_send.at[pl.ds(TY * i + 1, TY - 1)], ids_mid.at[i - 1], ids_ssem, im_recv.at[i - 1], across(i)),
        ]
    for copy in ids_copies:
        copy.start()

    for copy in loads[1:4]:
        copy.wait()

    def fill_table(c):
        share = frac[...]
        values = old[c]
        one = share * values
        high, low = split2(one)
        table[0:NBLK, 0:128] = high
        table[0:NBLK, 128:256] = low
        high, low = split2((1.0 - share) * values)
        table[NBLK : 2 * NBLK, 0:128] = high
        table[NBLK : 2 * NBLK, 128:256] = low

    def rows_copy(src, c, k, ssem, device):
        return remote(
            src, recv.at[c, pl.ds(slot_row(k), CAP), :], ssem, a2a_recv.at[c + (c // 3) * (k // 12)], device
        )

    def bundle_copy(c, i):
        src = send.at[c, pl.ds(CAP * (TY * i + 1), CAP * (TY - 1)), :]
        return remote(src, mid.at[c, i - 1], a2a_send.at[c], mid_recv.at[c, i - 1], across(i))

    def dispatch(c, g):
        both = jnp.dot(sel_src[g], table[...], preferred_element_type=F32)
        rows = both[:, 0:128] + both[:, 128:256]
        send[c, pl.ds(ROWS * g, ROWS), :] = rows
        i = g // 2
        if g == 0:
            recv[c, 0:CAP, :] = rows[0:CAP]
        elif g % 2 == 0:
            k = TY * i
            rows_copy(send.at[c, pl.ds(CAP * k, CAP), :], c, k, a2a_send.at[c], across(i)).start()
        if i == 0:
            for j in range(max(GROUP * g, 1), GROUP * (g + 1)):
                rows_copy(send.at[c, pl.ds(CAP * j, CAP), :], c, j, a2a_send.at[c], column(j)).start()
        elif g % 2 == 1:
            bundle_copy(c, i).start()

    def forward(c):
        for i in range(1, TX):
            bundle_copy(c, i).wait_recv()
            for j in range(1, TY):
                src = mid.at[c, i - 1, pl.ds(CAP * (j - 1), CAP), :]
                rows_copy(src, c, TY * i + j, fwd_send.at[c], column(j)).start()

    fill_table(0)
    for g in range(GROUPS):
        wanted = (ROWS * g + iota((ROWS, 1), 0)).astype(F32)
        code_of = jnp.sum(jnp.where(place == wanted, code, 0.0), axis=1, keepdims=True)
        hit = code_of.astype(jnp.int32) == iota((ROWS, OV), 1) + 1
        sel_src[g] = jnp.where(hit, 1.0, 0.0).astype(BF16)
        dispatch(0, g)

    def later(c, carry):
        fill_table(c)
        for g in range(GROUPS):
            dispatch(c, g)
        return carry

    for copy in panel_y:
        copy.wait()
    panel_x = [
        remote(pans.at[pl.ds(0, TY)], pans.at[pl.ds(TY * i, TY)], px_send.at[i - 1], px_recv.at[i - 1], across(i))
        for i in range(1, TX)
    ]
    for copy in panel_x:
        copy.start()
    for i in range(1, TX):
        ids_copies[TY - 1 + 2 * (i - 1) + 1].wait_recv()
        for j in range(1, TY):
            remote(ids_mid.at[i - 1, j - 1], ids_recv.at[TY * i + j], im_send, ids_rsem, column(j)).start()

    lax.fori_loop(1, COMPS - 1, later, 0)
    forward(0)
    lax.fori_loop(COMPS - 1, COMPS, later, 0)
    forward(1)

    for copy in disp_copies:
        copy.wait()
    nothing = jnp.zeros((8, CY), F32)
    for i, (c, d) in enumerate(PLANES):
        at = pl.ds(8 * i, 8)
        ext[c, 3:11, TOP - d, :] = jnp.where(at_left, nothing, xhl[at, :])
        ext[c, 3:11, TOP + CX - 1 + d, :] = jnp.where(at_right, nothing, xhr[at, :])

    @pl.when(at_bottom)
    def _():
        ext[:, 0:3, TOP : TOP + CX, :] = jnp.zeros((3, 3, CX, CY), F32)

    @pl.when(at_top)
    def _():
        ext[:, 3 + CZ : 6 + CZ, TOP : TOP + CX, :] = jnp.zeros((3, 3, CX, CY), F32)

    for corner in range(4):
        sz, sx = corner // 2, corner % 2
        outside = (at_bottom if sz else at_top) | (at_left if sx else at_right)
        for i, (c, dz, dx) in enumerate(LINES):
            z = -dz if sz else CZ - 1 + dz
            x = -dx if sx else CX - 1 + dx
            line = chl[corner, i]
            ext[c, 3 + z, pl.ds(TOP + x, 1), :] = jnp.where(outside, jnp.zeros_like(line), line)

    row = iota((32, CY), 0) - TOP
    keep_x = ((row >= 0) | jnp.logical_not(at_left)) & ((row < CX) | jnp.logical_not(at_right))

    def sweep(src, dst, c, zi):
        here = src[c, zi]
        near = src[c, zi + 1] + src[c, zi - 1]
        near = near + pltpu.roll(here, 1, 0) + pltpu.roll(here, 31, 0)
        near = near + ahead_y(here) + behind_y(here)
        new = here + relax_factor * (near / 6.0 - here)
        z = zi - 3
        inside = ((z >= 0) | jnp.logical_not(at_bottom)) & ((z < CZ) | jnp.logical_not(at_top))
        dst[c, zi] = jnp.where(keep_x & inside, new, 0.0)

    def first(zi, carry):
        for c in range(3):
            sweep(ext, s1, c, zi)
        return carry

    def second(zi, carry):
        for c in range(3):
            sweep(s1, ext, c, zi)
        return carry

    lax.fori_loop(1, 13, first, 0)
    lax.fori_loop(2, 12, second, 0)
    regrid_out = pltpu.make_async_copy(
        ext.at[:, pl.ds(3, CZ), pl.ds(TOP, CX), :], regrid_ref, out_sem.at[0]
    )
    regrid_out.start()

    def volumes(z, carry):
        zi = z + 3
        own = pl.ds(TOP, CX)
        stretch = ext[0, zi + 1, own, :] - ext[0, zi - 1, own, :]
        wide = ext[1, zi]
        wide = pltpu.roll(wide, 31, 0) - pltpu.roll(wide, 1, 0)
        along = ext[2, zi, own, :]
        stretch = stretch + wide[TOP : TOP + CX] + (ahead_y(along) - behind_y(along))
        vol[z] = 1.0 + cell_fraction * (0.5 * stretch)
        return carry

    lax.fori_loop(0, CZ, volumes, 0)

    for copy in panel_x:
        copy.wait()
    source = iota((N_TILE * 4, CX), 0)
    member = source // 4
    panel = ((tx + TX - member // TY) % TX) * (TY * 4) + (member % TY) * 4 + source % 4
    for yb in range(CY // 128):
        chosen = (panel == pids_ref[yb : yb + 1, :]) & (flags_ref[yb : yb + 1, :] != 0)
        chosen = jnp.where(chosen, 1.0, 0.0)
        for c in range(3):
            faces = pans[:, c].reshape(N_TILE * 4, 128)
            high, low = split2(faces)
            tn = (((0,), (0,)), ((), ()))
            weight = chosen.astype(BF16)
            got = lax.dot_general(weight, high, tn, preferred_element_type=F32)
            got = got + lax.dot_general(weight, low, tn, preferred_element_type=F32)
            trac[c, :, 128 * yb : 128 * (yb + 1)] = got

    forward(2)

    bulk = (N_TILE - 1) * CAP
    pltpu.make_async_copy(ids_recv.at[pl.ds(1, N_TILE - 1)], ids_recv.at[pl.ds(1, N_TILE - 1)], ids_rsem).wait()
    number = iota((NBLK, 128), 0).astype(F32) + 1.0
    for s in range(SETS):
        line = ids_recv[3 * s]
        for k in range(3 * s + 1, min(3 * s + 3, N_TILE)):
            line = line + ids_recv[k]
        sel_dst[:, 128 * s : 128 * (s + 1)] = jnp.where(number == line, 1.0, 0.0).astype(BF16)
    for s in range(SETS):
        used = CAP * min(3, N_TILE - 3 * s)
        for c in range(COMPS):
            recv[c, 128 * s + used : 128 * (s + 1), :] = jnp.zeros((128 - used, 128), F32)

    forward(3)

    def arrived(c, first, last, sem):
        rows = CAP * (min(3 * last, N_TILE) - max(3 * first, 1))
        pltpu.make_async_copy(recv.at[c, pl.ds(0, rows)], recv.at[c, pl.ds(0, rows)], sem).wait()
        at = pl.ds(128 * first, 128 * (last - first))
        high, low = split2(recv[c, at, :])
        both = jnp.dot(sel_dst[:, at], jnp.concatenate([high, low], axis=1), preferred_element_type=F32)
        return both[:, 0:128] + both[:, 128:256]

    def incoming(c):
        if c < 3:
            total = arrived(c, 0, SETS, a2a_recv.at[c])
        else:
            total = sum(arrived(c, *part, a2a_recv.at[c + i]) for i, part in enumerate(PARTS))
        return [total[128 * yb : 128 * (yb + 1)].reshape(CZ, CX, 128) for yb in range(CY // 128)]

    for copy in loads[4:]:
        copy.wait()
    for yb, more in enumerate(incoming(0)):
        at = pl.ds(128 * yb, 128)
        kmass[:, :, at] = kmass[:, :, at] + more

    spd_copies = []

    def send_speed(moves):
        for src, dst, dz, dx in moves:
            i = len(spd_copies)
            spd_copies.append(Shift(src, dst, sp_send.at[i], sp_recv.at[i], dz, dx))
            spd_copies[-1].start()

    change_x = jnp.zeros((CZ, CY), F32)
    for c in range(3):
        for yb, more in enumerate(incoming(c + 1)):
            at = pl.ds(128 * yb, 128)
            spd[c, 1 : 1 + CZ, :, at] = (kmom[c, :, :, at] + more) / kmass[:, :, at]
        first_x = spd[c, 1 : 1 + CZ, 0, :]
        last_x = spd[c, 1 : 1 + CZ, CX - 1, :]
        plane[c, 0:8, :] = first_x
        plane[c, 8:16, :] = last_x
        send_speed((
            (plane.at[c, pl.ds(0, 8), :], xp16.at[c, pl.ds(8, 8), :], 0, -1),
            (plane.at[c, pl.ds(8, 8), :], xm1.at[c, pl.ds(0, 8), :], 0, 1),
            (spd.at[c, CZ], spd.at[c, 0], 1, 0),
            (spd.at[c, pl.ds(1, 2)], spd.at[c, pl.ds(1 + CZ, 2)], -1, 0),
        ))
        change = spd[c, 1 : 1 + CZ, 1, :] - first_x
        change_x = change_x + change * change
        crs[0, c] = last_x[0:1]
        crs[1, c] = first_x[7:8]
        crs[2, c] = first_x[0:1]
    qst[...] = change_x
    send_speed((
        (qst, xq, 0, -1),
        (crs.at[0], crn.at[0], -1, 1),
        (crs.at[1], crn.at[1], 1, -1),
        (crs.at[2], crn.at[2], -1, -1),
    ))

    def squared(here, *others):
        total = jnp.zeros_like(here)
        for other in others:
            change = other - here
            total = total + change * change
        return total

    def viscosity(i, edge):
        squares = jnp.zeros((CX, CY), F32)
        for c in range(3):
            here = spd[c, i]
            row = here if edge is None else xp16[c, edge : edge + 1, :]
            squares = squares + squared(here, spd[c, i + 1], ahead_x(here, row), ahead_y(here))
        visc[i] = visc_of(squares)

    def pressure(z, edge):
        here = spd[0, z + 1]
        div = here - spd[0, z]
        here = spd[1, z + 1]
        div = div + (here - behind_x(here, here if edge is None else xm1[1, edge : edge + 1, :]))
        here = spd[2, z + 1]
        div = div + (here - behind_y(here))
        pres[z] = -penalty_factor * div

    lax.fori_loop(1, CZ, lambda i, carry: (viscosity(i, None), carry)[1], 0)
    lax.fori_loop(1, CZ, lambda z, carry: (pressure(z, None), carry)[1], 0)

    for copy in spd_copies:
        copy.wait()
    for c in range(3):
        xm1[c, 8:9, :] = crn[0, c]
        xp16[c, 7:8, :] = crn[1, c]
        xp16[c, 16:17, :] = crn[2, c]

    @pl.when(at_bottom)
    def _():
        for c in range(3):
            spd[c, 0] = jnp.zeros((CX, CY), F32)
            xp16[c, 0:8, :] = nothing

    @pl.when(at_top)
    def _():
        for c in range(3):
            spd[c, 1 + CZ : 3 + CZ] = jnp.zeros((2, CX, CY), F32)
            xm1[c, 8:16, :] = nothing
            xp16[c, 16:24, :] = nothing

    @pl.when(at_left)
    def _():
        for c in range(3):
            xm1[c] = jnp.zeros((16, CY), F32)

    @pl.when(at_right)
    def _():
        for c in range(3):
            xp16[c] = jnp.zeros((24, CY), F32)

    squares_m = jnp.zeros((CZ, CY), F32)
    squares_l = jnp.zeros((CZ, CY), F32)
    squares_p = xq[...]
    for c in range(3):
        whole = xm1[c]
        here = whole[0:8]
        above = pltpu.roll(whole, 15, 0)[0:8]
        squares_m = squares_m + squared(here, above, plane[c, 0:8, :], ahead_y(here))
        whole = xp16[c]
        here = whole[8:16]
        above = pltpu.roll(whole, 23, 0)[8:16]
        squares_p = squares_p + squared(here, above, ahead_y(here))
        last = plane[c, 8:16, :]
        above = ahead_x(last, spd[c, 1 + CZ, CX - 1 : CX, :])
        squares_l = squares_l + squared(last, above, here, ahead_y(last))
    side[0:8, :] = jnp.where(at_left, 0.0, visc_of(squares_m))
    side[8:16, :] = jnp.where(at_right, 0.0, visc_of(squares_p))
    here = xp16[0]
    div = here[8:16] - pltpu.roll(here, 1, 0)[8:16]
    div = div + (xp16[1, 8:16, :] - plane[1, 8:16, :])
    here = xp16[2, 8:16, :]
    div = div + (here - behind_y(here))
    side[16:24, :] = jnp.where(at_right, 0.0, -penalty_factor * div)
    here = plane[0, 0:8, :]
    div = here - behind_x(here, spd[0, 0, 0:1, :])
    div = div + (plane[1, 0:8, :] - xm1[1, 0:8, :])
    here = plane[2, 0:8, :]
    div = div + (here - behind_y(here))

    viscosity(0, 7)
    viscosity(CZ, 15)
    viscosity(CZ + 1, 16)
    pressure(0, 0)
    pressure(CZ, 8)
    visc[1 : 1 + CZ, CX - 1, :] = visc_of(squares_l)
    pres[0:CZ, 0, :] = -penalty_factor * div

    @pl.when(at_bottom)
    def _():
        visc[0] = jnp.zeros((CX, CY), F32)

    @pl.when(at_top)
    def _():
        visc[CZ + 1] = jnp.zeros((CX, CY), F32)
        pres[CZ] = jnp.zeros((CX, CY), F32)

    def update(z, carry):
        v = visc[z + 1]
        line = pl.ds(z, 1)
        v_next = (visc[z + 2], ahead_x(v, side[pl.ds(z + 8, 1), :]), ahead_y(v))
        v_prev = (visc[z], behind_x(v, side[line, :]), behind_y(v))
        forward = [0.5 * (v + other) for other in v_next]
        backward = [0.5 * (v + other) for other in v_prev]
        density = kmass[z] / vol[z]
        bottom = forward[0] + backward[0] + forward[1] + backward[1] + forward[2] + backward[2] + density
        p = pres[z]
        p_next = (pres[z + 1], ahead_x(p, side[pl.ds(z + 16, 1), :]), ahead_y(p))
        for c in range(3):
            here = spd[c, z + 1]
            top = forward[0] * spd[c, z + 2] + backward[0] * spd[c, z]
            top = top + forward[1] * ahead_x(here, xp16[c, pl.ds(z + 8, 1), :])
            top = top + backward[1] * behind_x(here, xm1[c, line, :])
            top = top + forward[2] * ahead_y(here) + backward[2] * behind_y(here)
            top = top - (p_next[c] - p) + trac[c] + density * here
            vel_ref[c, z] = top / bottom
        return carry

    lax.fori_loop(0, CZ, update, 0)

    for c in range(COMPS):
        pltpu.make_async_copy(send.at[c, pl.ds(0, bulk)], send.at[c, pl.ds(0, bulk)], a2a_send.at[c]).wait()
        pltpu.make_async_copy(mid.at[c], mid.at[c], fwd_send.at[c]).wait()
    pltpu.make_async_copy(ids_send.at[pl.ds(1, N_TILE - 1)], ids_send.at[pl.ds(1, N_TILE - 1)], ids_ssem).wait()
    pltpu.make_async_copy(ids_mid, ids_mid, im_send).wait()
    regrid_out.wait()


def store(regrid_ref, vel_ref, regrid_hbm, vel_hbm, sem):
    copies = [
        pltpu.make_async_copy(regrid_ref, regrid_hbm, sem.at[0]),
        pltpu.make_async_copy(vel_ref, vel_hbm, sem.at[1]),
    ]
    for copy in copies:
        copy.start()
    for copy in copies:
        copy.wait()


def shards(
    displacement, old_mass, old_momentum, intersection_fraction, entry_order, target_owner,
    target_block, kept_mass, kept_momentum, surface_panels, panel_ids, contact_flags,
):
    grid = jax.ShapeDtypeStruct((3, CZ, CX, CY), F32)
    hbm, vmem = pl.BlockSpec(memory_space=pltpu.HBM), pl.BlockSpec(memory_space=pltpu.VMEM)
    dma = pltpu.SemaphoreType.DMA
    regridded, velocity = pl.pallas_call(
        kernel,
        out_shape=(pltpu.VMEM(grid.shape, F32), pltpu.VMEM(grid.shape, F32)),
        in_specs=[hbm] * 12,
        out_specs=(vmem, vmem),
        scratch_shapes=[
            pltpu.VMEM((1, OV), jnp.int32),
            pltpu.VMEM((1, OV), jnp.int32),
            pltpu.VMEM((1, OV), jnp.int32),
            pltpu.VMEM((3, 4, 128), F32),
            pltpu.VMEM((4, CX), jnp.int32),
            pltpu.VMEM((4, CX), jnp.int32),
            pltpu.VMEM((3, CZ + 6, 32, CY), F32),
            pltpu.VMEM((3, CZ + 6, 32, CY), F32),
            pltpu.VMEM((COMPS, NBLK, 128), F32),
            pltpu.VMEM((NBLK, 128), F32),
            pltpu.VMEM((CZ, CX, CY), F32),
            pltpu.VMEM((3, CZ, CX, CY), F32),
            pltpu.VMEM((CZ, CX, CY), F32),
            pltpu.VMEM((GROUPS, ROWS, OV), BF16),
            pltpu.VMEM((2 * NBLK, 256), BF16),
            pltpu.VMEM((COMPS, N_TILE * CAP, 128), F32),
            pltpu.VMEM((COMPS, TX - 1, CAP * (TY - 1), 128), F32),
            pltpu.VMEM((COMPS, RROWS, 128), F32),
            pltpu.VMEM((N_TILE, 1, 128), F32),
            pltpu.VMEM((TX - 1, TY - 1, 1, 128), F32),
            pltpu.VMEM((N_TILE, 1, 128), F32),
            pltpu.VMEM((NBLK, RROWS), BF16),
            pltpu.VMEM((2, 8 * len(PLANES), CY), F32),
            pltpu.VMEM((8 * len(PLANES), CY), F32),
            pltpu.VMEM((8 * len(PLANES), CY), F32),
            pltpu.VMEM((4, len(LINES), 1, CY), F32),
            pltpu.VMEM((4, len(LINES), 1, CY), F32),
            pltpu.VMEM((N_TILE, 3, 4, 128), F32),
            pltpu.VMEM((3, CX, CY), F32),
            pltpu.VMEM((3, CZ + 3, CX, CY), F32),
            pltpu.VMEM((3, 16, CY), F32),
            pltpu.VMEM((3, 16, CY), F32),
            pltpu.VMEM((3, 24, CY), F32),
            pltpu.VMEM((8, CY), F32),
            pltpu.VMEM((8, CY), F32),
            pltpu.VMEM((3, 3, 1, CY), F32),
            pltpu.VMEM((3, 3, 1, CY), F32),
            pltpu.VMEM((24, CY), F32),
            pltpu.VMEM((CZ + 2, CX, CY), F32),
            pltpu.VMEM((CZ + 1, CX, CY), F32),
            dma((6,)),
            dma((6,)),
            dma((1,)),
            dma((COMPS,)),
            dma((COMPS - 1 + len(PARTS),)),
            dma((COMPS, TX - 1)),
            dma((COMPS,)),
            dma,
            dma,
            dma,
            dma((TX - 1,)),
            dma((8,)),
            dma((8,)),
            dma((TY - 1,)),
            dma((TY - 1,)),
            dma((TX - 1,)),
            dma((TX - 1,)),
            dma((16,)),
            dma((16,)),
        ],
        compiler_params=pltpu.CompilerParams(
            collective_id=0, has_side_effects=True, vmem_limit_bytes=48 * 2**20
        ),
    )(
        *(
            pltpu.with_memory_space_constraint(value, pltpu.HBM)
            for value in (
                displacement,
                old_mass,
                old_momentum.transpose(1, 0, 2),
                intersection_fraction,
                entry_order,
                target_owner.reshape(1, OV),
                target_block.reshape(1, OV),
                kept_mass,
                kept_momentum,
                surface_panels.transpose(1, 0, 2),
                panel_ids[0].T,
                contact_flags[0].T,
            )
        )
    )
    return pl.pallas_call(
        store,
        out_shape=(grid, grid),
        in_specs=[vmem, vmem],
        out_specs=(hbm, hbm),
        scratch_shapes=[dma((2,))],
        compiler_params=pltpu.CompilerParams(vmem_limit_bytes=2**20),
    )(*(pltpu.with_memory_space_constraint(value, pltpu.VMEM) for value in (regridded, velocity)))


def solution(mesh):
    return jax.shard_map(
        shards,
        mesh=mesh,
        in_specs=(
            P(None, "band", "tile", None),
            P(("band", "tile"), None),
            P(("band", "tile"), None, None),
            P(("band", "tile"), None),
            P(("band", "tile"), None),
            P(("band", "tile"), None),
            P(("band", "tile")),
            P("band", "tile", None),
            P(None, "band", "tile", None),
            P(("band", "tile"), None, None),
            P("band", "tile", None),
            P("band", "tile", None),
        ),
        out_specs=(P(None, "band", "tile", None), P(None, "band", "tile", None)),
        check_vma=False,
    )
```

```python
import jax
import jax.numpy as jnp
from jax import lax
from jax.experimental import pallas as pl
from jax.experimental.pallas import tpu as pltpu
from jax.sharding import PartitionSpec as P

MESH = pl.DeviceIdType.MESH
F32, BF16 = jnp.float32, jnp.bfloat16

relax_factor = 0.8
cell_fraction = 0.1
strain_eps = 0.05
rate_power = -0.4
penalty_factor = 0.5

N_BAND, N_TILE = 16, 32
TX, TY = 4, 8
CZ, CX, CY = 8, 16, 512
OV, NBLK, CAP = 1024, 512, 40
COMPS = 4
GROUP = 4
GROUPS = N_TILE // GROUP
ROWS = GROUP * CAP
SETS = (N_TILE + 2) // 3
RROWS = SETS * 128
TOP = 8
PLANES = ((0, 1), (0, 2), (1, 1), (1, 2), (1, 3), (2, 1), (2, 2))
LINES = ((0, 1, 1), (0, 1, 2), (0, 2, 1), (1, 1, 1), (1, 1, 2), (1, 2, 1), (2, 1, 1))
PARTS = ((0, 4), (4, 8), (8, SETS))


def slot_row(k):
    return 128 * (k // 3) + CAP * (k % 3)


def split2(value):
    high = value.astype(BF16)
    low = (value - high.astype(F32)).astype(BF16)
    return high, low


def iota(shape, dim):
    return lax.broadcasted_iota(jnp.int32, shape, dim)


def ahead_y(f):
    n = f.shape[-1]
    return jnp.where(iota(f.shape, f.ndim - 1) == n - 1, 0.0, pltpu.roll(f, n - 1, f.ndim - 1))


def behind_y(f):
    return jnp.where(iota(f.shape, f.ndim - 1) == 0, 0.0, pltpu.roll(f, 1, f.ndim - 1))


def ahead_x(f, row):
    n = f.shape[0]
    return jnp.where(iota(f.shape, 0) == n - 1, row, pltpu.roll(f, n - 1, 0))


def behind_x(f, row):
    return jnp.where(iota(f.shape, 0) == 0, row, pltpu.roll(f, 1, 0))


def visc_of(squares):
    return jnp.exp(rate_power * jnp.log(strain_eps + squares))


def kernel(
    disp_hbm, mass_hbm, mom_hbm, frac_hbm, order_hbm, owner_hbm, block_hbm,
    kmass_hbm, kmom_hbm, panels_hbm, pids_hbm, flags_hbm,
    regrid_ref, spd, xm1, xp16, side, visc, pres, dens, trac,
    order_ref, owner_ref, block_ref, panels_ref, pids_ref, flags_ref,
    ext, s1, old, frac, kmass, kmom, vol, sel_src, table, send, mid, recv, ids_send, ids_mid, ids_recv,
    sel_dst, xst, xhl, xhr, cst, chl, pans, plane, qst, xq, crs, crn,
    small_sem, load_sem, out_sem, a2a_send, a2a_recv, mid_recv, fwd_send, ids_ssem, ids_rsem, im_send, im_recv, dh_send, dh_recv,
    py_send, py_recv, px_send, px_recv, sp_send, sp_recv,
):
    b = lax.axis_index("band")
    t = lax.axis_index("tile")
    tx, ty = t // TY, t % TY
    up, down = (b + 1) % N_BAND, (b + N_BAND - 1) % N_BAND
    right, left = (t + 1) % N_TILE, (t + N_TILE - 1) % N_TILE

    def peer(k):
        i = k // TY
        return ((tx + (i ^ (i >> 1))) % TX) * TY + (ty + k % TY) % TY

    barrier = pltpu.get_barrier_semaphore()
    partners = [(b, peer(j)) for j in range(1, TY)] + [(b, peer(TY * i)) for i in range(1, TX)]
    for partner in partners:
        pl.semaphore_signal(barrier, inc=1, device_id=partner, device_id_type=MESH)
    at_left, at_right = t == 0, t == N_TILE - 1
    at_bottom, at_top = b == 0, b == N_BAND - 1

    def there(dz, dx):
        z_end = at_top if dz > 0 else at_bottom if dz < 0 else False
        x_end = at_right if dx > 0 else at_left if dx < 0 else False
        return jnp.logical_not(jnp.logical_or(z_end, x_end))

    def neighbour(dz, dx):
        return (up if dz > 0 else down if dz < 0 else b, right if dx > 0 else left if dx < 0 else t)

    around = [(dz, dx) for dz in (-1, 0, 1) for dx in (-1, 0, 1) if (dz, dx) != (0, 0)]
    greeted = len(partners)
    for way in around:

        @pl.when(there(*way))
        def _():
            pl.semaphore_signal(barrier, inc=1, device_id=neighbour(*way), device_id_type=MESH)

        greeted = greeted + there(*way).astype(jnp.int32)

    small = [(owner_hbm, owner_ref), (order_hbm, order_ref), (block_hbm, block_ref),
             (panels_hbm, panels_ref), (pids_hbm, pids_ref), (flags_hbm, flags_ref)]
    small = [pltpu.make_async_copy(src, dst, small_sem.at[i]) for i, (src, dst) in enumerate(small)]
    loads = [
        pltpu.make_async_copy(disp_hbm, ext.at[:, pl.ds(3, CZ), pl.ds(TOP, CX), :], load_sem.at[0]),
        pltpu.make_async_copy(frac_hbm, frac, load_sem.at[1]),
        pltpu.make_async_copy(mass_hbm, old.at[0], load_sem.at[2]),
        pltpu.make_async_copy(mom_hbm, old.at[pl.ds(1, 3)], load_sem.at[3]),
        pltpu.make_async_copy(kmass_hbm, kmass, load_sem.at[4]),
        pltpu.make_async_copy(kmom_hbm, kmom, load_sem.at[5]),
    ]
    for copy in small + loads[1:4] + loads[:1] + loads[4:]:
        copy.start()

    for copy in small:
        copy.wait()
    owner = owner_ref[...]
    column = iota((N_TILE, 1), 0)
    steps = column // TY
    column_dest = ((tx + (steps ^ (steps >> 1))) % TX) * TY + (ty + column % TY) % TY
    before = (iota((128, 128), 0) < iota((128, 128), 1)).astype(BF16)
    base = jnp.zeros((N_TILE, 1), F32)
    slots, names = [], []
    for j in range(OV // 128):
        hot = (owner[:, 128 * j : 128 * (j + 1)] == column_dest).astype(F32)
        prefix = base + jnp.dot(hot.astype(BF16), before, preferred_element_type=F32)
        slots.append(jnp.sum(hot * prefix, axis=0, keepdims=True))
        names.append(jnp.sum(hot * column.astype(F32), axis=0, keepdims=True))
        base = base + jnp.sum(hot, axis=1, keepdims=True)
    slot = jnp.concatenate(slots, axis=1)
    name = jnp.concatenate(names, axis=1)
    place = name * CAP + slot
    order = order_ref[...]
    code = (order // 2 + (order % 2) * NBLK + 1).astype(F32)


    def remote(src, dst, ssem, rsem, device):
        return pltpu.make_async_remote_copy(
            src_ref=src, dst_ref=dst, send_sem=ssem, recv_sem=rsem, device_id=device, device_id_type=MESH
        )

    def column(j):
        return (b, peer(j))

    def across(i):
        return (b, peer(TY * i))

    for copy in loads[1:4]:
        copy.wait()

    def fill_table(c):
        share = frac[...]
        values = old[c]
        one = share * values
        high, low = split2(one)
        table[0:NBLK, 0:128] = high
        table[0:NBLK, 128:256] = low
        high, low = split2((1.0 - share) * values)
        table[NBLK : 2 * NBLK, 0:128] = high
        table[NBLK : 2 * NBLK, 128:256] = low

    def rows_copy(src, c, k, ssem, device):
        return remote(
            src, recv.at[c, pl.ds(slot_row(k), CAP), :], ssem, a2a_recv.at[c + (c // 3) * (k // 12)], device
        )

    def bundle_copy(c, i):
        src = send.at[c, pl.ds(CAP * (TY * i + 1), CAP * (TY - 1)), :]
        return remote(src, mid.at[c, i - 1], a2a_send.at[c], mid_recv.at[c, i - 1], across(i))

    def dispatch(c, g):
        both = jnp.dot(sel_src[g], table[...], preferred_element_type=F32)
        rows = both[:, 0:128] + both[:, 128:256]
        send[c, pl.ds(ROWS * g, ROWS), :] = rows
        i = g // 2
        if g == 0:
            recv[c, 0:CAP, :] = rows[0:CAP]
        elif g % 2 == 0:
            k = TY * i
            rows_copy(send.at[c, pl.ds(CAP * k, CAP), :], c, k, a2a_send.at[c], across(i)).start()
        if i == 0:
            for j in range(max(GROUP * g, 1), GROUP * (g + 1)):
                rows_copy(send.at[c, pl.ds(CAP * j, CAP), :], c, j, a2a_send.at[c], column(j)).start()
        elif g % 2 == 1:
            bundle_copy(c, i).start()

    def forward(c):
        for i in range(1, TX):
            bundle_copy(c, i).wait_recv()
            for j in range(1, TY):
                src = mid.at[c, i - 1, pl.ds(CAP * (j - 1), CAP), :]
                rows_copy(src, c, TY * i + j, fwd_send.at[c], column(j)).start()

    fill_table(0)
    pl.semaphore_wait(barrier, greeted)
    for g in range(GROUPS):
        wanted = (ROWS * g + iota((ROWS, 1), 0)).astype(F32)
        code_of = jnp.sum(jnp.where(place == wanted, code, 0.0), axis=1, keepdims=True)
        hit = code_of.astype(jnp.int32) == iota((ROWS, OV), 1) + 1
        sel_src[g] = jnp.where(hit, 1.0, 0.0).astype(BF16)
        dispatch(0, g)

    block = block_ref[...]
    target = (block % 4) * 128 + block // 4 + 1
    hot = owner == column_dest
    high = jnp.where(hot, target // 16, 0).astype(F32).astype(BF16)
    low = jnp.where(hot, target % 16, 0).astype(F32).astype(BF16)
    lanes = (slot == iota((128, 1), 0).astype(F32)).astype(F32).astype(BF16)
    dims = (((1,), (1,)), ((), ()))
    ids = 16.0 * lax.dot_general(high, lanes, dims, preferred_element_type=F32)
    ids = ids + lax.dot_general(low, lanes, dims, preferred_element_type=F32)
    third = iota((N_TILE, 128), 0) % 3
    ids = jnp.where(
        third == 0, ids, jnp.where(third == 1, pltpu.roll(ids, CAP, 1), pltpu.roll(ids, 2 * CAP, 1))
    )
    for k in range(N_TILE):
        ids_send[k] = ids[k : k + 1, :]
    ids_recv[0] = ids[0:1, :]


    ids_copies = [remote(ids_send.at[j], ids_recv.at[j], ids_ssem, ids_rsem, column(j)) for j in range(1, TY)]
    for i in range(1, TX):
        ids_copies += [
            remote(ids_send.at[TY * i], ids_recv.at[TY * i], ids_ssem, ids_rsem, across(i)),
            remote(ids_send.at[pl.ds(TY * i + 1, TY - 1)], ids_mid.at[i - 1], ids_ssem, im_recv.at[i - 1], across(i)),
        ]
    for copy in ids_copies:
        copy.start()

    loads[0].wait()
    for i, (c, d) in enumerate(PLANES):
        at = pl.ds(8 * i, 8)
        xst[0, at, :] = ext[c, 3:11, TOP + CX - d, :]
        xst[1, at, :] = ext[c, 3:11, TOP + d - 1, :]
    for corner in range(4):
        sz, sx = corner // 2, corner % 2
        for i, (c, dz, dx) in enumerate(LINES):
            z = CZ - dz if sz else dz - 1
            x = CX - dx if sx else dx - 1
            cst[corner, i] = ext[c, 3 + z, pl.ds(TOP + x, 1), :]
    pans[ty] = panels_ref[...]

    class Shift:
        def __init__(self, src, dst, ssem, rsem, dz, dx):
            self.copy = remote(src, dst, ssem, rsem, neighbour(dz, dx))
            self.goes, self.comes = there(dz, dx), there(-dz, -dx)

        def start(self):
            pl.when(self.goes)(self.copy.start)

        def wait(self):
            pl.when(self.goes)(self.copy.wait_send)
            pl.when(self.comes)(self.copy.wait_recv)

    disp_copies = [
        Shift(xst.at[0], xhl, dh_send.at[0], dh_recv.at[0], 0, 1),
        Shift(xst.at[1], xhr, dh_send.at[1], dh_recv.at[1], 0, -1),
        Shift(disp_hbm.at[:, pl.ds(CZ - 3, 3)], ext.at[:, pl.ds(0, 3), pl.ds(TOP, CX), :],
              dh_send.at[2], dh_recv.at[2], 1, 0),
        Shift(disp_hbm.at[:, pl.ds(0, 3)], ext.at[:, pl.ds(3 + CZ, 3), pl.ds(TOP, CX), :],
              dh_send.at[3], dh_recv.at[3], -1, 0),
    ]
    for corner in range(4):
        sz, sx = corner // 2, corner % 2
        disp_copies.append(
            Shift(cst.at[corner], chl.at[corner], dh_send.at[4 + corner], dh_recv.at[4 + corner],
                  1 if sz else -1, 1 if sx else -1)
        )
    for copy in disp_copies:
        copy.start()
    panel_y = [
        remote(pans.at[ty], pans.at[ty], py_send.at[i - 1], py_recv.at[i - 1], (b, tx * TY + (ty + i) % TY))
        for i in range(1, TY)
    ]
    for copy in panel_y:
        copy.start()

    def later(c, carry):
        fill_table(c)
        for g in range(GROUPS):
            dispatch(c, g)
        return carry

    lax.fori_loop(1, COMPS - 1, later, 0)
    for copy in panel_y:
        copy.wait()
    panel_x = [
        remote(pans.at[pl.ds(0, TY)], pans.at[pl.ds(TY * i, TY)], px_send.at[i - 1], px_recv.at[i - 1], across(i))
        for i in range(1, TX)
    ]
    for copy in panel_x:
        copy.start()
    for i in range(1, TX):
        ids_copies[TY - 1 + 2 * (i - 1) + 1].wait_recv()
        for j in range(1, TY):
            remote(ids_mid.at[i - 1, j - 1], ids_recv.at[TY * i + j], im_send, ids_rsem, column(j)).start()

    forward(0)
    lax.fori_loop(COMPS - 1, COMPS, later, 0)
    forward(1)

    for copy in disp_copies:
        copy.wait()
    nothing = jnp.zeros((8, CY), F32)
    for i, (c, d) in enumerate(PLANES):
        at = pl.ds(8 * i, 8)
        ext[c, 3:11, TOP - d, :] = jnp.where(at_left, nothing, xhl[at, :])
        ext[c, 3:11, TOP + CX - 1 + d, :] = jnp.where(at_right, nothing, xhr[at, :])

    @pl.when(at_bottom)
    def _():
        ext[:, 0:3, TOP : TOP + CX, :] = jnp.zeros((3, 3, CX, CY), F32)

    @pl.when(at_top)
    def _():
        ext[:, 3 + CZ : 6 + CZ, TOP : TOP + CX, :] = jnp.zeros((3, 3, CX, CY), F32)

    for corner in range(4):
        sz, sx = corner // 2, corner % 2
        outside = (at_bottom if sz else at_top) | (at_left if sx else at_right)
        for i, (c, dz, dx) in enumerate(LINES):
            z = -dz if sz else CZ - 1 + dz
            x = -dx if sx else CX - 1 + dx
            line = chl[corner, i]
            ext[c, 3 + z, pl.ds(TOP + x, 1), :] = jnp.where(outside, jnp.zeros_like(line), line)

    row = iota((32, CY), 0) - TOP
    keep_x = ((row >= 0) | jnp.logical_not(at_left)) & ((row < CX) | jnp.logical_not(at_right))

    def sweep(src, dst, c, zi):
        here = src[c, zi]
        near = src[c, zi + 1] + src[c, zi - 1]
        near = near + pltpu.roll(here, 1, 0) + pltpu.roll(here, 31, 0)
        near = near + ahead_y(here) + behind_y(here)
        new = here + relax_factor * (near / 6.0 - here)
        z = zi - 3
        inside = ((z >= 0) | jnp.logical_not(at_bottom)) & ((z < CZ) | jnp.logical_not(at_top))
        dst[c, zi] = jnp.where(keep_x & inside, new, 0.0)

    def first(zi, carry):
        for c in range(3):
            sweep(ext, s1, c, zi)
        return carry

    def second(zi, carry):
        for c in range(3):
            sweep(s1, ext, c, zi)
        return carry

    lax.fori_loop(1, 13, first, 0)
    lax.fori_loop(2, 12, second, 0)
    regrid_out = pltpu.make_async_copy(
        ext.at[:, pl.ds(3, CZ), pl.ds(TOP, CX), :], regrid_ref, out_sem.at[0]
    )
    regrid_out.start()

    def volumes(z, carry):
        zi = z + 3
        own = pl.ds(TOP, CX)
        stretch = ext[0, zi + 1, own, :] - ext[0, zi - 1, own, :]
        wide = ext[1, zi]
        wide = pltpu.roll(wide, 31, 0) - pltpu.roll(wide, 1, 0)
        along = ext[2, zi, own, :]
        stretch = stretch + wide[TOP : TOP + CX] + (ahead_y(along) - behind_y(along))
        vol[z] = 1.0 + cell_fraction * (0.5 * stretch)
        return carry

    lax.fori_loop(0, CZ, volumes, 0)

    for copy in panel_x:
        copy.wait()
    source = iota((N_TILE * 4, CX), 0)
    member = source // 4
    steps = member // TY
    panel = ((tx + TX - (steps ^ (steps >> 1))) % TX) * (TY * 4) + (member % TY) * 4 + source % 4
    for yb in range(CY // 128):
        chosen = (panel == pids_ref[yb : yb + 1, :]) & (flags_ref[yb : yb + 1, :] != 0)
        chosen = jnp.where(chosen, 1.0, 0.0)
        for c in range(3):
            faces = pans[:, c].reshape(N_TILE * 4, 128)
            high, low = split2(faces)
            tn = (((0,), (0,)), ((), ()))
            weight = chosen.astype(BF16)
            got = lax.dot_general(weight, high, tn, preferred_element_type=F32)
            got = got + lax.dot_general(weight, low, tn, preferred_element_type=F32)
            trac[c, :, 128 * yb : 128 * (yb + 1)] = got

    forward(2)

    bulk = (N_TILE - 1) * CAP
    pltpu.make_async_copy(ids_recv.at[pl.ds(1, N_TILE - 1)], ids_recv.at[pl.ds(1, N_TILE - 1)], ids_rsem).wait()
    number = iota((NBLK, 128), 0).astype(F32) + 1.0
    for s in range(SETS):
        line = ids_recv[3 * s]
        for k in range(3 * s + 1, min(3 * s + 3, N_TILE)):
            line = line + ids_recv[k]
        sel_dst[:, 128 * s : 128 * (s + 1)] = jnp.where(number == line, 1.0, 0.0).astype(BF16)
    for s in range(SETS):
        used = CAP * min(3, N_TILE - 3 * s)
        for c in range(COMPS):
            recv[c, 128 * s + used : 128 * (s + 1), :] = jnp.zeros((128 - used, 128), F32)

    forward(3)

    def arrived(c, first, last, sem):
        rows = CAP * (min(3 * last, N_TILE) - max(3 * first, 1))
        pltpu.make_async_copy(recv.at[c, pl.ds(0, rows)], recv.at[c, pl.ds(0, rows)], sem).wait()
        at = pl.ds(128 * first, 128 * (last - first))
        high, low = split2(recv[c, at, :])
        both = jnp.dot(sel_dst[:, at], jnp.concatenate([high, low], axis=1), preferred_element_type=F32)
        return both[:, 0:128] + both[:, 128:256]

    def incoming(c):
        if c < 3:
            total = arrived(c, 0, SETS, a2a_recv.at[c])
        else:
            total = sum(arrived(c, *part, a2a_recv.at[c + i]) for i, part in enumerate(PARTS))
        return [total[128 * yb : 128 * (yb + 1)].reshape(CZ, CX, 128) for yb in range(CY // 128)]

    for copy in loads[4:]:
        copy.wait()
    for yb, more in enumerate(incoming(0)):
        at = pl.ds(128 * yb, 128)
        mass = kmass[:, :, at] + more
        dens[:, :, at] = mass / vol[:, :, at]
        kmass[:, :, at] = 1.0 / mass

    spd_copies = []

    def send_speed(moves):
        for src, dst, dz, dx in moves:
            i = len(spd_copies)
            spd_copies.append(Shift(src, dst, sp_send.at[i], sp_recv.at[i], dz, dx))
            spd_copies[-1].start()

    change_x = jnp.zeros((CZ, CY), F32)
    for c in range(3):
        for yb, more in enumerate(incoming(c + 1)):
            at = pl.ds(128 * yb, 128)
            spd[c, 1 : 1 + CZ, :, at] = (kmom[c, :, :, at] + more) * kmass[:, :, at]
        first_x = spd[c, 1 : 1 + CZ, 0, :]
        last_x = spd[c, 1 : 1 + CZ, CX - 1, :]
        plane[c, 0:8, :] = first_x
        plane[c, 8:16, :] = last_x
        send_speed((
            (plane.at[c, pl.ds(0, 8), :], xp16.at[c, pl.ds(8, 8), :], 0, -1),
            (plane.at[c, pl.ds(8, 8), :], xm1.at[c, pl.ds(0, 8), :], 0, 1),
            (spd.at[c, CZ], spd.at[c, 0], 1, 0),
            (spd.at[c, pl.ds(1, 2)], spd.at[c, pl.ds(1 + CZ, 2)], -1, 0),
        ))
        change = spd[c, 1 : 1 + CZ, 1, :] - first_x
        change_x = change_x + change * change
        crs[0, c] = last_x[0:1]
        crs[1, c] = first_x[7:8]
        crs[2, c] = first_x[0:1]
    qst[...] = change_x
    send_speed((
        (qst, xq, 0, -1),
        (crs.at[0], crn.at[0], -1, 1),
        (crs.at[1], crn.at[1], 1, -1),
        (crs.at[2], crn.at[2], -1, -1),
    ))

    def squared(here, *others):
        total = jnp.zeros_like(here)
        for other in others:
            change = other - here
            total = total + change * change
        return total

    def viscosity(i, edge):
        squares = jnp.zeros((CX, CY), F32)
        for c in range(3):
            here = spd[c, i]
            row = here if edge is None else xp16[c, edge : edge + 1, :]
            squares = squares + squared(here, spd[c, i + 1], ahead_x(here, row), ahead_y(here))
        visc[i] = visc_of(squares)

    def pressure(z, edge):
        here = spd[0, z + 1]
        div = here - spd[0, z]
        here = spd[1, z + 1]
        div = div + (here - behind_x(here, here if edge is None else xm1[1, edge : edge + 1, :]))
        here = spd[2, z + 1]
        div = div + (here - behind_y(here))
        pres[z] = -penalty_factor * div

    lax.fori_loop(1, CZ, lambda i, carry: (viscosity(i, None), carry)[1], 0)
    lax.fori_loop(1, CZ, lambda z, carry: (pressure(z, None), carry)[1], 0)

    for copy in spd_copies:
        copy.wait()
    for c in range(3):
        xm1[c, 8:9, :] = crn[0, c]
        xp16[c, 7:8, :] = crn[1, c]
        xp16[c, 16:17, :] = crn[2, c]

    @pl.when(at_bottom)
    def _():
        for c in range(3):
            spd[c, 0] = jnp.zeros((CX, CY), F32)
            xp16[c, 0:8, :] = nothing

    @pl.when(at_top)
    def _():
        for c in range(3):
            spd[c, 1 + CZ : 3 + CZ] = jnp.zeros((2, CX, CY), F32)
            xm1[c, 8:16, :] = nothing
            xp16[c, 16:24, :] = nothing

    @pl.when(at_left)
    def _():
        for c in range(3):
            xm1[c] = jnp.zeros((16, CY), F32)

    @pl.when(at_right)
    def _():
        for c in range(3):
            xp16[c] = jnp.zeros((24, CY), F32)

    squares_m = jnp.zeros((CZ, CY), F32)
    squares_l = jnp.zeros((CZ, CY), F32)
    squares_p = xq[...]
    for c in range(3):
        whole = xm1[c]
        here = whole[0:8]
        above = pltpu.roll(whole, 15, 0)[0:8]
        squares_m = squares_m + squared(here, above, plane[c, 0:8, :], ahead_y(here))
        whole = xp16[c]
        here = whole[8:16]
        above = pltpu.roll(whole, 23, 0)[8:16]
        squares_p = squares_p + squared(here, above, ahead_y(here))
        last = plane[c, 8:16, :]
        above = ahead_x(last, spd[c, 1 + CZ, CX - 1 : CX, :])
        squares_l = squares_l + squared(last, above, here, ahead_y(last))
    side[0:8, :] = jnp.where(at_left, 0.0, visc_of(squares_m))
    side[8:16, :] = jnp.where(at_right, 0.0, visc_of(squares_p))
    here = xp16[0]
    div = here[8:16] - pltpu.roll(here, 1, 0)[8:16]
    div = div + (xp16[1, 8:16, :] - plane[1, 8:16, :])
    here = xp16[2, 8:16, :]
    div = div + (here - behind_y(here))
    side[16:24, :] = jnp.where(at_right, 0.0, -penalty_factor * div)
    here = plane[0, 0:8, :]
    div = here - behind_x(here, spd[0, 0, 0:1, :])
    div = div + (plane[1, 0:8, :] - xm1[1, 0:8, :])
    here = plane[2, 0:8, :]
    div = div + (here - behind_y(here))

    viscosity(0, 7)
    viscosity(CZ, 15)
    viscosity(CZ + 1, 16)
    pressure(0, 0)
    pressure(CZ, 8)
    visc[1 : 1 + CZ, CX - 1, :] = visc_of(squares_l)
    pres[0:CZ, 0, :] = -penalty_factor * div

    @pl.when(at_bottom)
    def _():
        visc[0] = jnp.zeros((CX, CY), F32)

    @pl.when(at_top)
    def _():
        visc[CZ + 1] = jnp.zeros((CX, CY), F32)
        pres[CZ] = jnp.zeros((CX, CY), F32)

    for c in range(COMPS):
        pltpu.make_async_copy(send.at[c, pl.ds(0, bulk)], send.at[c, pl.ds(0, bulk)], a2a_send.at[c]).wait()
        pltpu.make_async_copy(mid.at[c], mid.at[c], fwd_send.at[c]).wait()
    pltpu.make_async_copy(ids_send.at[pl.ds(1, N_TILE - 1)], ids_send.at[pl.ds(1, N_TILE - 1)], ids_ssem).wait()
    pltpu.make_async_copy(ids_mid, ids_mid, im_send).wait()
    regrid_out.wait()


def finish(regrid_ref, spd, xm1, xp16, side, visc, pres, dens, trac, regrid_hbm, vel_hbm, vel, sem):
    regrid_out = pltpu.make_async_copy(regrid_ref, regrid_hbm, sem.at[CZ])
    regrid_out.start()

    def update(z, carry):
        v = visc[z + 1]
        line = pl.ds(z, 1)
        v_next = (visc[z + 2], ahead_x(v, side[pl.ds(z + 8, 1), :]), ahead_y(v))
        v_prev = (visc[z], behind_x(v, side[line, :]), behind_y(v))
        forward = [0.5 * (v + other) for other in v_next]
        backward = [0.5 * (v + other) for other in v_prev]
        density = dens[z]
        bottom = forward[0] + backward[0] + forward[1] + backward[1] + forward[2] + backward[2] + density
        p = pres[z]
        p_next = (pres[z + 1], ahead_x(p, side[pl.ds(z + 16, 1), :]), ahead_y(p))
        for c in range(3):
            here = spd[c, z + 1]
            top = forward[0] * spd[c, z + 2] + backward[0] * spd[c, z]
            top = top + forward[1] * ahead_x(here, xp16[c, pl.ds(z + 8, 1), :])
            top = top + backward[1] * behind_x(here, xm1[c, line, :])
            top = top + forward[2] * ahead_y(here) + backward[2] * behind_y(here)
            top = top - (p_next[c] - p) + trac[c] + density * here
            vel[c, z] = top / bottom
        pltpu.make_async_copy(vel.at[:, z], vel_hbm.at[:, z], sem.at[z]).start()
        return carry

    lax.fori_loop(0, CZ, update, 0)
    for z in range(CZ):
        pltpu.make_async_copy(vel.at[:, z], vel_hbm.at[:, z], sem.at[z]).wait()
    regrid_out.wait()


def shards(
    displacement, old_mass, old_momentum, intersection_fraction, entry_order, target_owner,
    target_block, kept_mass, kept_momentum, surface_panels, panel_ids, contact_flags,
):
    grid = jax.ShapeDtypeStruct((3, CZ, CX, CY), F32)
    hbm, vmem = pl.BlockSpec(memory_space=pltpu.HBM), pl.BlockSpec(memory_space=pltpu.VMEM)
    dma = pltpu.SemaphoreType.DMA
    parts = (
        (3, CZ, CX, CY),
        (3, CZ + 3, CX, CY),
        (3, 16, CY),
        (3, 24, CY),
        (24, CY),
        (CZ + 2, CX, CY),
        (CZ + 1, CX, CY),
        (CZ, CX, CY),
        (3, CX, CY),
    )
    fields = pl.pallas_call(
        kernel,
        out_shape=[pltpu.VMEM(part, F32) for part in parts],
        in_specs=[hbm] * 12,
        out_specs=[vmem] * len(parts),
        scratch_shapes=[
            pltpu.VMEM((1, OV), jnp.int32),
            pltpu.VMEM((1, OV), jnp.int32),
            pltpu.VMEM((1, OV), jnp.int32),
            pltpu.VMEM((3, 4, 128), F32),
            pltpu.VMEM((4, CX), jnp.int32),
            pltpu.VMEM((4, CX), jnp.int32),
            pltpu.VMEM((3, CZ + 6, 32, CY), F32),
            pltpu.VMEM((3, CZ + 6, 32, CY), F32),
            pltpu.VMEM((COMPS, NBLK, 128), F32),
            pltpu.VMEM((NBLK, 128), F32),
            pltpu.VMEM((CZ, CX, CY), F32),
            pltpu.VMEM((3, CZ, CX, CY), F32),
            pltpu.VMEM((CZ, CX, CY), F32),
            pltpu.VMEM((GROUPS, ROWS, OV), BF16),
            pltpu.VMEM((2 * NBLK, 256), BF16),
            pltpu.VMEM((COMPS, N_TILE * CAP, 128), F32),
            pltpu.VMEM((COMPS, TX - 1, CAP * (TY - 1), 128), F32),
            pltpu.VMEM((COMPS, RROWS, 128), F32),
            pltpu.VMEM((N_TILE, 1, 128), F32),
            pltpu.VMEM((TX - 1, TY - 1, 1, 128), F32),
            pltpu.VMEM((N_TILE, 1, 128), F32),
            pltpu.VMEM((NBLK, RROWS), BF16),
            pltpu.VMEM((2, 8 * len(PLANES), CY), F32),
            pltpu.VMEM((8 * len(PLANES), CY), F32),
            pltpu.VMEM((8 * len(PLANES), CY), F32),
            pltpu.VMEM((4, len(LINES), 1, CY), F32),
            pltpu.VMEM((4, len(LINES), 1, CY), F32),
            pltpu.VMEM((N_TILE, 3, 4, 128), F32),
            pltpu.VMEM((3, 16, CY), F32),
            pltpu.VMEM((8, CY), F32),
            pltpu.VMEM((8, CY), F32),
            pltpu.VMEM((3, 3, 1, CY), F32),
            pltpu.VMEM((3, 3, 1, CY), F32),
            dma((6,)),
            dma((6,)),
            dma((1,)),
            dma((COMPS,)),
            dma((COMPS - 1 + len(PARTS),)),
            dma((COMPS, TX - 1)),
            dma((COMPS,)),
            dma,
            dma,
            dma,
            dma((TX - 1,)),
            dma((8,)),
            dma((8,)),
            dma((TY - 1,)),
            dma((TY - 1,)),
            dma((TX - 1,)),
            dma((TX - 1,)),
            dma((16,)),
            dma((16,)),
        ],
        compiler_params=pltpu.CompilerParams(
            collective_id=0, has_side_effects=True, vmem_limit_bytes=48 * 2**20
        ),
    )(
        *(
            pltpu.with_memory_space_constraint(value, pltpu.HBM)
            for value in (
                displacement,
                old_mass,
                old_momentum.transpose(1, 0, 2),
                intersection_fraction,
                entry_order,
                target_owner.reshape(1, OV),
                target_block.reshape(1, OV),
                kept_mass,
                kept_momentum,
                surface_panels.transpose(1, 0, 2),
                panel_ids[0].T,
                contact_flags[0].T,
            )
        )
    )
    return pl.pallas_call(
        finish,
        out_shape=(grid, grid),
        in_specs=[vmem] * len(parts),
        out_specs=(hbm, hbm),
        scratch_shapes=[pltpu.VMEM(grid.shape, F32), dma((CZ + 1,))],
        compiler_params=pltpu.CompilerParams(vmem_limit_bytes=4 * 2**20),
    )(*(pltpu.with_memory_space_constraint(field, pltpu.VMEM) for field in fields))


def solution(mesh):
    return jax.shard_map(
        shards,
        mesh=mesh,
        in_specs=(
            P(None, "band", "tile", None),
            P(("band", "tile"), None),
            P(("band", "tile"), None, None),
            P(("band", "tile"), None),
            P(("band", "tile"), None),
            P(("band", "tile"), None),
            P(("band", "tile")),
            P("band", "tile", None),
            P(None, "band", "tile", None),
            P(("band", "tile"), None, None),
            P("band", "tile", None),
            P("band", "tile", None),
        ),
        out_specs=(P(None, "band", "tile", None), P(None, "band", "tile", None)),
        check_vma=False,
    )
```

```python
import jax
import jax.numpy as jnp
from jax import lax
from jax.experimental import pallas as pl
from jax.experimental.pallas import tpu as pltpu
from jax.sharding import PartitionSpec as P

MESH = pl.DeviceIdType.MESH
F32, BF16 = jnp.float32, jnp.bfloat16

relax_factor = 0.8
cell_fraction = 0.1
strain_eps = 0.05
rate_power = -0.4
penalty_factor = 0.5

N_BAND, N_TILE = 16, 32
TX, TY = 4, 8
CZ, CX, CY = 8, 16, 512
OV, NBLK, CAP = 1024, 512, 40
COMPS = 4
GROUP = 4
GROUPS = N_TILE // GROUP
ROWS = GROUP * CAP
SETS = (N_TILE + 2) // 3
RROWS = SETS * 128
TOP = 8
PLANES = ((0, 1), (0, 2), (1, 1), (1, 2), (1, 3), (2, 1), (2, 2))
LINES = ((0, 1, 1), (0, 1, 2), (0, 2, 1), (1, 1, 1), (1, 1, 2), (1, 2, 1), (2, 1, 1))
PARTS = ((0, 4), (4, 8), (8, SETS))


def slot_row(k):
    return 128 * (k // 3) + CAP * (k % 3)


def split2(value):
    high = value.astype(BF16)
    low = (value - high.astype(F32)).astype(BF16)
    return high, low


def iota(shape, dim):
    return lax.broadcasted_iota(jnp.int32, shape, dim)


def ahead_y(f):
    n = f.shape[-1]
    return jnp.where(iota(f.shape, f.ndim - 1) == n - 1, 0.0, pltpu.roll(f, n - 1, f.ndim - 1))


def behind_y(f):
    return jnp.where(iota(f.shape, f.ndim - 1) == 0, 0.0, pltpu.roll(f, 1, f.ndim - 1))


def ahead_x(f, row):
    n = f.shape[0]
    return jnp.where(iota(f.shape, 0) == n - 1, row, pltpu.roll(f, n - 1, 0))


def behind_x(f, row):
    return jnp.where(iota(f.shape, 0) == 0, row, pltpu.roll(f, 1, 0))


def visc_of(squares):
    return jnp.exp(rate_power * jnp.log(strain_eps + squares))


def kernel(
    disp_hbm, mass_hbm, mom_hbm, frac_hbm, order_hbm, owner_hbm, block_hbm,
    kmass_hbm, kmom_hbm, panels_hbm, pids_hbm, flags_hbm,
    regrid_ref, spd, xm1, xp16, side, visc, pres, dens, trac, vel,
    order_ref, owner_ref, block_ref, panels_ref, pids_ref, flags_ref,
    ext, s1, old, frac, kmass, kmom, vol, sel_src, table, send, mid, recv, ids_send, ids_mid, ids_recv,
    sel_dst, xst, xhl, xhr, cst, chl, pans, plane, qst, xq, crs, crn,
    small_sem, load_sem, out_sem, a2a_send, a2a_recv, mid_recv, fwd_send, ids_ssem, ids_rsem, im_send, im_recv, dh_send, dh_recv,
    py_send, py_recv, px_send, px_recv, sp_send, sp_recv,
):
    b = lax.axis_index("band")
    t = lax.axis_index("tile")
    tx, ty = t // TY, t % TY
    up, down = (b + 1) % N_BAND, (b + N_BAND - 1) % N_BAND
    right, left = (t + 1) % N_TILE, (t + N_TILE - 1) % N_TILE

    def peer(k):
        i = k // TY
        return ((tx + (i ^ (i >> 1))) % TX) * TY + (ty + k % TY) % TY

    barrier = pltpu.get_barrier_semaphore()
    partners = [(b, peer(j)) for j in range(1, TY)] + [(b, peer(TY * i)) for i in range(1, TX)]
    for partner in partners:
        pl.semaphore_signal(barrier, inc=1, device_id=partner, device_id_type=MESH)
    at_left, at_right = t == 0, t == N_TILE - 1
    at_bottom, at_top = b == 0, b == N_BAND - 1

    def there(dz, dx):
        z_end = at_top if dz > 0 else at_bottom if dz < 0 else False
        x_end = at_right if dx > 0 else at_left if dx < 0 else False
        return jnp.logical_not(jnp.logical_or(z_end, x_end))

    def neighbour(dz, dx):
        return (up if dz > 0 else down if dz < 0 else b, right if dx > 0 else left if dx < 0 else t)

    around = [(dz, dx) for dz in (-1, 0, 1) for dx in (-1, 0, 1) if (dz, dx) != (0, 0)]
    greeted = len(partners)
    for way in around:

        @pl.when(there(*way))
        def _():
            pl.semaphore_signal(barrier, inc=1, device_id=neighbour(*way), device_id_type=MESH)

        greeted = greeted + there(*way).astype(jnp.int32)

    small = [(owner_hbm, owner_ref), (order_hbm, order_ref), (block_hbm, block_ref),
             (panels_hbm, panels_ref), (pids_hbm, pids_ref), (flags_hbm, flags_ref)]
    small = [pltpu.make_async_copy(src, dst, small_sem.at[i]) for i, (src, dst) in enumerate(small)]
    loads = [
        pltpu.make_async_copy(disp_hbm, ext.at[:, pl.ds(3, CZ), pl.ds(TOP, CX), :], load_sem.at[0]),
        pltpu.make_async_copy(frac_hbm, frac, load_sem.at[1]),
        pltpu.make_async_copy(mass_hbm, old.at[0], load_sem.at[2]),
        pltpu.make_async_copy(mom_hbm, old.at[pl.ds(1, 3)], load_sem.at[3]),
        pltpu.make_async_copy(kmass_hbm, kmass, load_sem.at[4]),
        pltpu.make_async_copy(kmom_hbm, kmom, load_sem.at[5]),
    ]
    for copy in small + loads[1:4] + loads[:1] + loads[4:]:
        copy.start()

    for copy in small:
        copy.wait()
    owner = owner_ref[...]
    column = iota((N_TILE, 1), 0)
    steps = column // TY
    column_dest = ((tx + (steps ^ (steps >> 1))) % TX) * TY + (ty + column % TY) % TY
    before = (iota((128, 128), 0) < iota((128, 128), 1)).astype(BF16)
    base = jnp.zeros((N_TILE, 1), F32)
    slots, names = [], []
    for j in range(OV // 128):
        hot = (owner[:, 128 * j : 128 * (j + 1)] == column_dest).astype(F32)
        prefix = base + jnp.dot(hot.astype(BF16), before, preferred_element_type=F32)
        slots.append(jnp.sum(hot * prefix, axis=0, keepdims=True))
        names.append(jnp.sum(hot * column.astype(F32), axis=0, keepdims=True))
        base = base + jnp.sum(hot, axis=1, keepdims=True)
    slot = jnp.concatenate(slots, axis=1)
    name = jnp.concatenate(names, axis=1)
    place = name * CAP + slot
    order = order_ref[...]
    code = (order // 2 + (order % 2) * NBLK + 1).astype(F32)


    def remote(src, dst, ssem, rsem, device):
        return pltpu.make_async_remote_copy(
            src_ref=src, dst_ref=dst, send_sem=ssem, recv_sem=rsem, device_id=device, device_id_type=MESH
        )

    def column(j):
        return (b, peer(j))

    def across(i):
        return (b, peer(TY * i))

    for copy in loads[1:4]:
        copy.wait()

    def fill_table(c):
        share = frac[...]
        values = old[c]
        one = share * values
        high, low = split2(one)
        table[0:NBLK, 0:128] = high
        table[0:NBLK, 128:256] = low
        high, low = split2((1.0 - share) * values)
        table[NBLK : 2 * NBLK, 0:128] = high
        table[NBLK : 2 * NBLK, 128:256] = low

    def rows_copy(src, c, k, ssem, device):
        return remote(
            src, recv.at[c, pl.ds(slot_row(k), CAP), :], ssem, a2a_recv.at[c + (c // 3) * (k // 12)], device
        )

    def bundle_copy(c, i):
        src = send.at[c, pl.ds(CAP * (TY * i + 1), CAP * (TY - 1)), :]
        return remote(src, mid.at[c, i - 1], a2a_send.at[c], mid_recv.at[c, i - 1], across(i))

    def dispatch(c, g):
        both = jnp.dot(sel_src[g], table[...], preferred_element_type=F32)
        rows = both[:, 0:128] + both[:, 128:256]
        send[c, pl.ds(ROWS * g, ROWS), :] = rows
        i = g // 2
        if g == 0:
            recv[c, 0:CAP, :] = rows[0:CAP]
        elif g % 2 == 0:
            k = TY * i
            rows_copy(send.at[c, pl.ds(CAP * k, CAP), :], c, k, a2a_send.at[c], across(i)).start()
        if i == 0:
            for j in range(max(GROUP * g, 1), GROUP * (g + 1)):
                rows_copy(send.at[c, pl.ds(CAP * j, CAP), :], c, j, a2a_send.at[c], column(j)).start()
        elif g % 2 == 1:
            bundle_copy(c, i).start()

    def forward(c):
        for i in range(1, TX):
            bundle_copy(c, i).wait_recv()
            for j in range(1, TY):
                src = mid.at[c, i - 1, pl.ds(CAP * (j - 1), CAP), :]
                rows_copy(src, c, TY * i + j, fwd_send.at[c], column(j)).start()

    fill_table(0)
    pl.semaphore_wait(barrier, greeted)
    for g in range(GROUPS):
        wanted = (ROWS * g + iota((ROWS, 1), 0)).astype(F32)
        code_of = jnp.sum(jnp.where(place == wanted, code, 0.0), axis=1, keepdims=True)
        hit = code_of.astype(jnp.int32) == iota((ROWS, OV), 1) + 1
        sel_src[g] = jnp.where(hit, 1.0, 0.0).astype(BF16)
        dispatch(0, g)

    block = block_ref[...]
    target = (block % 4) * 128 + block // 4 + 1
    hot = owner == column_dest
    high = jnp.where(hot, target // 16, 0).astype(F32).astype(BF16)
    low = jnp.where(hot, target % 16, 0).astype(F32).astype(BF16)
    lanes = (slot == iota((128, 1), 0).astype(F32)).astype(F32).astype(BF16)
    dims = (((1,), (1,)), ((), ()))
    ids = 16.0 * lax.dot_general(high, lanes, dims, preferred_element_type=F32)
    ids = ids + lax.dot_general(low, lanes, dims, preferred_element_type=F32)
    third = iota((N_TILE, 128), 0) % 3
    ids = jnp.where(
        third == 0, ids, jnp.where(third == 1, pltpu.roll(ids, CAP, 1), pltpu.roll(ids, 2 * CAP, 1))
    )
    for k in range(N_TILE):
        ids_send[k] = ids[k : k + 1, :]
    ids_recv[0] = ids[0:1, :]


    ids_copies = [remote(ids_send.at[j], ids_recv.at[j], ids_ssem, ids_rsem, column(j)) for j in range(1, TY)]
    for i in range(1, TX):
        ids_copies += [
            remote(ids_send.at[TY * i], ids_recv.at[TY * i], ids_ssem, ids_rsem, across(i)),
            remote(ids_send.at[pl.ds(TY * i + 1, TY - 1)], ids_mid.at[i - 1], ids_ssem, im_recv.at[i - 1], across(i)),
        ]
    for copy in ids_copies:
        copy.start()

    loads[0].wait()
    for i, (c, d) in enumerate(PLANES):
        at = pl.ds(8 * i, 8)
        xst[0, at, :] = ext[c, 3:11, TOP + CX - d, :]
        xst[1, at, :] = ext[c, 3:11, TOP + d - 1, :]
    for corner in range(4):
        sz, sx = corner // 2, corner % 2
        for i, (c, dz, dx) in enumerate(LINES):
            z = CZ - dz if sz else dz - 1
            x = CX - dx if sx else dx - 1
            cst[corner, i] = ext[c, 3 + z, pl.ds(TOP + x, 1), :]
    pans[ty] = panels_ref[...]

    class Shift:
        def __init__(self, src, dst, ssem, rsem, dz, dx):
            self.copy = remote(src, dst, ssem, rsem, neighbour(dz, dx))
            self.goes, self.comes, self.flat = there(dz, dx), there(-dz, -dx), dz == 0

        def start(self):
            pl.when(self.goes)(self.copy.start)

        def wait(self):
            pl.when(self.goes)(self.copy.wait_send)
            pl.when(self.comes)(self.copy.wait_recv)

    disp_copies = [
        Shift(xst.at[0], xhl, dh_send.at[0], dh_recv.at[0], 0, 1),
        Shift(xst.at[1], xhr, dh_send.at[1], dh_recv.at[1], 0, -1),
        Shift(disp_hbm.at[:, pl.ds(CZ - 3, 3)], ext.at[:, pl.ds(0, 3), pl.ds(TOP, CX), :],
              dh_send.at[2], dh_recv.at[2], 1, 0),
        Shift(disp_hbm.at[:, pl.ds(0, 3)], ext.at[:, pl.ds(3 + CZ, 3), pl.ds(TOP, CX), :],
              dh_send.at[3], dh_recv.at[3], -1, 0),
    ]
    for corner in range(4):
        sz, sx = corner // 2, corner % 2
        disp_copies.append(
            Shift(cst.at[corner], chl.at[corner], dh_send.at[4 + corner], dh_recv.at[4 + corner],
                  1 if sz else -1, 1 if sx else -1)
        )
    for copy in disp_copies:
        copy.start()
    panel_y = [
        remote(pans.at[ty], pans.at[ty], py_send.at[i - 1], py_recv.at[i - 1], (b, tx * TY + (ty + i) % TY))
        for i in range(1, TY)
    ]
    for copy in panel_y:
        copy.start()

    def later(c, carry):
        fill_table(c)
        for g in range(GROUPS):
            dispatch(c, g)
        return carry

    lax.fori_loop(1, COMPS - 1, later, 0)
    for copy in panel_y:
        copy.wait()
    panel_x = [
        remote(pans.at[pl.ds(0, TY)], pans.at[pl.ds(TY * i, TY)], px_send.at[i - 1], px_recv.at[i - 1], across(i))
        for i in range(1, TX)
    ]
    for copy in panel_x:
        copy.start()
    for i in range(1, TX):
        ids_copies[TY - 1 + 2 * (i - 1) + 1].wait_recv()
        for j in range(1, TY):
            remote(ids_mid.at[i - 1, j - 1], ids_recv.at[TY * i + j], im_send, ids_rsem, column(j)).start()

    forward(0)
    lax.fori_loop(COMPS - 1, COMPS, later, 0)
    forward(1)

    for copy in disp_copies:
        copy.wait()
    nothing = jnp.zeros((8, CY), F32)
    for i, (c, d) in enumerate(PLANES):
        at = pl.ds(8 * i, 8)
        ext[c, 3:11, TOP - d, :] = jnp.where(at_left, nothing, xhl[at, :])
        ext[c, 3:11, TOP + CX - 1 + d, :] = jnp.where(at_right, nothing, xhr[at, :])

    @pl.when(at_bottom)
    def _():
        ext[:, 0:3, TOP : TOP + CX, :] = jnp.zeros((3, 3, CX, CY), F32)

    @pl.when(at_top)
    def _():
        ext[:, 3 + CZ : 6 + CZ, TOP : TOP + CX, :] = jnp.zeros((3, 3, CX, CY), F32)

    for corner in range(4):
        sz, sx = corner // 2, corner % 2
        outside = (at_bottom if sz else at_top) | (at_left if sx else at_right)
        for i, (c, dz, dx) in enumerate(LINES):
            z = -dz if sz else CZ - 1 + dz
            x = -dx if sx else CX - 1 + dx
            line = chl[corner, i]
            ext[c, 3 + z, pl.ds(TOP + x, 1), :] = jnp.where(outside, jnp.zeros_like(line), line)

    row = iota((32, CY), 0) - TOP
    keep_x = ((row >= 0) | jnp.logical_not(at_left)) & ((row < CX) | jnp.logical_not(at_right))

    def sweep(src, dst, c, zi):
        here = src[c, zi]
        near = src[c, zi + 1] + src[c, zi - 1]
        near = near + pltpu.roll(here, 1, 0) + pltpu.roll(here, 31, 0)
        near = near + ahead_y(here) + behind_y(here)
        new = here + relax_factor * (near / 6.0 - here)
        z = zi - 3
        inside = ((z >= 0) | jnp.logical_not(at_bottom)) & ((z < CZ) | jnp.logical_not(at_top))
        dst[c, zi] = jnp.where(keep_x & inside, new, 0.0)

    def first(zi, carry):
        for c in range(3):
            sweep(ext, s1, c, zi)
        return carry

    def second(zi, carry):
        for c in range(3):
            sweep(s1, ext, c, zi)
        return carry

    lax.fori_loop(1, 13, first, 0)
    lax.fori_loop(2, 12, second, 0)
    regrid_out = pltpu.make_async_copy(
        ext.at[:, pl.ds(3, CZ), pl.ds(TOP, CX), :], regrid_ref, out_sem.at[0]
    )
    regrid_out.start()

    def volumes(z, carry):
        zi = z + 3
        own = pl.ds(TOP, CX)
        stretch = ext[0, zi + 1, own, :] - ext[0, zi - 1, own, :]
        wide = ext[1, zi]
        wide = pltpu.roll(wide, 31, 0) - pltpu.roll(wide, 1, 0)
        along = ext[2, zi, own, :]
        stretch = stretch + wide[TOP : TOP + CX] + (ahead_y(along) - behind_y(along))
        vol[z] = 1.0 + cell_fraction * (0.5 * stretch)
        return carry

    lax.fori_loop(0, CZ, volumes, 0)

    for copy in panel_x:
        copy.wait()
    source = iota((N_TILE * 4, CX), 0)
    member = source // 4
    steps = member // TY
    panel = ((tx + TX - (steps ^ (steps >> 1))) % TX) * (TY * 4) + (member % TY) * 4 + source % 4
    for yb in range(CY // 128):
        chosen = (panel == pids_ref[yb : yb + 1, :]) & (flags_ref[yb : yb + 1, :] != 0)
        chosen = jnp.where(chosen, 1.0, 0.0)
        for c in range(3):
            faces = pans[:, c].reshape(N_TILE * 4, 128)
            high, low = split2(faces)
            tn = (((0,), (0,)), ((), ()))
            weight = chosen.astype(BF16)
            got = lax.dot_general(weight, high, tn, preferred_element_type=F32)
            got = got + lax.dot_general(weight, low, tn, preferred_element_type=F32)
            trac[c, :, 128 * yb : 128 * (yb + 1)] = got

    forward(2)

    bulk = (N_TILE - 1) * CAP
    pltpu.make_async_copy(ids_recv.at[pl.ds(1, N_TILE - 1)], ids_recv.at[pl.ds(1, N_TILE - 1)], ids_rsem).wait()
    number = iota((NBLK, 128), 0).astype(F32) + 1.0
    for s in range(SETS):
        line = ids_recv[3 * s]
        for k in range(3 * s + 1, min(3 * s + 3, N_TILE)):
            line = line + ids_recv[k]
        sel_dst[:, 128 * s : 128 * (s + 1)] = jnp.where(number == line, 1.0, 0.0).astype(BF16)
    for s in range(SETS):
        used = CAP * min(3, N_TILE - 3 * s)
        for c in range(COMPS):
            recv[c, 128 * s + used : 128 * (s + 1), :] = jnp.zeros((128 - used, 128), F32)

    forward(3)

    def arrived(c, first, last, sem):
        rows = CAP * (min(3 * last, N_TILE) - max(3 * first, 1))
        pltpu.make_async_copy(recv.at[c, pl.ds(0, rows)], recv.at[c, pl.ds(0, rows)], sem).wait()
        at = pl.ds(128 * first, 128 * (last - first))
        high, low = split2(recv[c, at, :])
        both = jnp.dot(sel_dst[:, at], jnp.concatenate([high, low], axis=1), preferred_element_type=F32)
        return both[:, 0:128] + both[:, 128:256]

    def incoming(c):
        if c < 3:
            total = arrived(c, 0, SETS, a2a_recv.at[c])
        else:
            total = sum(arrived(c, *part, a2a_recv.at[c + i]) for i, part in enumerate(PARTS))
        return [total[128 * yb : 128 * (yb + 1)].reshape(CZ, CX, 128) for yb in range(CY // 128)]

    for copy in loads[4:]:
        copy.wait()
    for yb, more in enumerate(incoming(0)):
        at = pl.ds(128 * yb, 128)
        mass = kmass[:, :, at] + more
        dens[:, :, at] = mass / vol[:, :, at]
        kmass[:, :, at] = 1.0 / mass

    spd_copies = []

    def send_speed(moves):
        for src, dst, dz, dx in moves:
            i = len(spd_copies)
            spd_copies.append(Shift(src, dst, sp_send.at[i], sp_recv.at[i], dz, dx))
            spd_copies[-1].start()

    change_x = jnp.zeros((CZ, CY), F32)
    for c in range(3):
        for yb, more in enumerate(incoming(c + 1)):
            at = pl.ds(128 * yb, 128)
            spd[c, 1 : 1 + CZ, :, at] = (kmom[c, :, :, at] + more) * kmass[:, :, at]
        first_x = spd[c, 1 : 1 + CZ, 0, :]
        last_x = spd[c, 1 : 1 + CZ, CX - 1, :]
        plane[c, 0:8, :] = first_x
        plane[c, 8:16, :] = last_x
        send_speed((
            (plane.at[c, pl.ds(0, 8), :], xp16.at[c, pl.ds(8, 8), :], 0, -1),
            (plane.at[c, pl.ds(8, 8), :], xm1.at[c, pl.ds(0, 8), :], 0, 1),
            (spd.at[c, CZ], spd.at[c, 0], 1, 0),
            (spd.at[c, pl.ds(1, 2)], spd.at[c, pl.ds(1 + CZ, 2)], -1, 0),
        ))
        change = spd[c, 1 : 1 + CZ, 1, :] - first_x
        change_x = change_x + change * change
        crs[0, c] = last_x[0:1]
        crs[1, c] = first_x[7:8]
        crs[2, c] = first_x[0:1]
    qst[...] = change_x
    send_speed((
        (qst, xq, 0, -1),
        (crs.at[0], crn.at[0], -1, 1),
        (crs.at[1], crn.at[1], 1, -1),
        (crs.at[2], crn.at[2], -1, -1),
    ))

    def squared(here, *others):
        total = jnp.zeros_like(here)
        for other in others:
            change = other - here
            total = total + change * change
        return total

    def viscosity(i, edge):
        squares = jnp.zeros((CX, CY), F32)
        for c in range(3):
            here = spd[c, i]
            row = here if edge is None else xp16[c, edge : edge + 1, :]
            squares = squares + squared(here, spd[c, i + 1], ahead_x(here, row), ahead_y(here))
        visc[i] = visc_of(squares)

    def pressure(z, edge):
        here = spd[0, z + 1]
        div = here - spd[0, z]
        here = spd[1, z + 1]
        div = div + (here - behind_x(here, here if edge is None else xm1[1, edge : edge + 1, :]))
        here = spd[2, z + 1]
        div = div + (here - behind_y(here))
        pres[z] = -penalty_factor * div

    lax.fori_loop(1, CZ, lambda i, carry: (viscosity(i, None), carry)[1], 0, unroll=7)
    lax.fori_loop(1, CZ, lambda z, carry: (pressure(z, None), carry)[1], 0)

    def x_ends():
        @pl.when(at_left)
        def _():
            for c in range(3):
                xm1[c] = jnp.zeros((16, CY), F32)

        @pl.when(at_right)
        def _():
            for c in range(3):
                xp16[c] = jnp.zeros((24, CY), F32)

    def lines(final):
        squares_m = jnp.zeros((CZ, CY), F32)
        squares_l = jnp.zeros((CZ, CY), F32)
        squares_p = xq[...]
        for c in range(3):
            whole = xm1[c]
            here = whole[0:8]
            above = pltpu.roll(whole, 15, 0)[0:8]
            squares_m = squares_m + squared(here, above, plane[c, 0:8, :], ahead_y(here))
            whole = xp16[c]
            here = whole[8:16]
            above = pltpu.roll(whole, 23, 0)[8:16]
            squares_p = squares_p + squared(here, above, ahead_y(here))
            last = plane[c, 8:16, :]
            above = ahead_x(last, spd[c, 1 + CZ, CX - 1 : CX, :] if final else last)
            squares_l = squares_l + squared(last, above, here, ahead_y(last))
        side[0:8, :] = jnp.where(at_left, 0.0, visc_of(squares_m))
        side[8:16, :] = jnp.where(at_right, 0.0, visc_of(squares_p))
        here = xp16[0]
        div = here[8:16] - pltpu.roll(here, 1, 0)[8:16]
        div = div + (xp16[1, 8:16, :] - plane[1, 8:16, :])
        here = xp16[2, 8:16, :]
        div = div + (here - behind_y(here))
        side[16:24, :] = jnp.where(at_right, 0.0, -penalty_factor * div)
        here = plane[0, 0:8, :]
        div = here - behind_x(here, spd[0, 0, 0:1, :] if final else here)
        div = div + (plane[1, 0:8, :] - xm1[1, 0:8, :])
        here = plane[2, 0:8, :]
        div = div + (here - behind_y(here))
        visc[1 : 1 + CZ, CX - 1, :] = visc_of(squares_l)
        pres[0:CZ, 0, :] = -penalty_factor * div

    for copy in spd_copies:
        if copy.flat:
            copy.wait()
    x_ends()
    lines(False)
    for z in range(1, CZ - 2):
        update(z, vel, spd, xm1, xp16, side, visc, pres, dens, trac)

    for copy in spd_copies:
        if not copy.flat:
            copy.wait()
    for c in range(3):
        xm1[c, 8:9, :] = crn[0, c]
        xp16[c, 7:8, :] = crn[1, c]
        xp16[c, 16:17, :] = crn[2, c]
    x_ends()

    @pl.when(at_bottom)
    def _():
        for c in range(3):
            spd[c, 0] = jnp.zeros((CX, CY), F32)
            xp16[c, 0:8, :] = nothing

    @pl.when(at_top)
    def _():
        for c in range(3):
            spd[c, 1 + CZ : 3 + CZ] = jnp.zeros((2, CX, CY), F32)
            xm1[c, 8:16, :] = nothing
            xp16[c, 16:24, :] = nothing

    viscosity(0, 7)
    viscosity(CZ, 15)
    viscosity(CZ + 1, 16)
    pressure(0, 0)
    pressure(CZ, 8)
    lines(True)

    @pl.when(at_bottom)
    def _():
        visc[0] = jnp.zeros((CX, CY), F32)

    @pl.when(at_top)
    def _():
        visc[CZ + 1] = jnp.zeros((CX, CY), F32)
        pres[CZ] = jnp.zeros((CX, CY), F32)

    for c in range(COMPS):
        pltpu.make_async_copy(send.at[c, pl.ds(0, bulk)], send.at[c, pl.ds(0, bulk)], a2a_send.at[c]).wait()
        pltpu.make_async_copy(mid.at[c], mid.at[c], fwd_send.at[c]).wait()
    pltpu.make_async_copy(ids_send.at[pl.ds(1, N_TILE - 1)], ids_send.at[pl.ds(1, N_TILE - 1)], ids_ssem).wait()
    pltpu.make_async_copy(ids_mid, ids_mid, im_send).wait()
    regrid_out.wait()


def update(z, vel, spd, xm1, xp16, side, visc, pres, dens, trac):
    v = visc[z + 1]
    line = pl.ds(z, 1)
    v_next = (visc[z + 2], ahead_x(v, side[pl.ds(z + 8, 1), :]), ahead_y(v))
    v_prev = (visc[z], behind_x(v, side[line, :]), behind_y(v))
    forward = [0.5 * (v + other) for other in v_next]
    backward = [0.5 * (v + other) for other in v_prev]
    density = dens[z]
    bottom = forward[0] + backward[0] + forward[1] + backward[1] + forward[2] + backward[2] + density
    p = pres[z]
    p_next = (pres[z + 1], ahead_x(p, side[pl.ds(z + 16, 1), :]), ahead_y(p))
    for c in range(3):
        here = spd[c, z + 1]
        top = forward[0] * spd[c, z + 2] + backward[0] * spd[c, z]
        top = top + forward[1] * ahead_x(here, xp16[c, pl.ds(z + 8, 1), :])
        top = top + backward[1] * behind_x(here, xm1[c, line, :])
        top = top + forward[2] * ahead_y(here) + backward[2] * behind_y(here)
        top = top - (p_next[c] - p) + trac[c] + density * here
        vel[c, z] = top / bottom


def finish(regrid_ref, spd, xm1, xp16, side, visc, pres, dens, trac, vel, regrid_hbm, vel_hbm, late, sem):
    early = pl.ds(1, CZ - 3)
    copies = [
        pltpu.make_async_copy(vel.at[:, early], vel_hbm.at[:, early], sem.at[CZ]),
        pltpu.make_async_copy(regrid_ref, regrid_hbm, sem.at[CZ + 1]),
    ]
    for copy in copies:
        copy.start()
    for z in (0, CZ - 2, CZ - 1):
        update(z, late, spd, xm1, xp16, side, visc, pres, dens, trac)
        copies.append(pltpu.make_async_copy(late.at[:, z], vel_hbm.at[:, z], sem.at[z]))
        copies[-1].start()
    for copy in copies:
        copy.wait()


def shards(
    displacement, old_mass, old_momentum, intersection_fraction, entry_order, target_owner,
    target_block, kept_mass, kept_momentum, surface_panels, panel_ids, contact_flags,
):
    grid = jax.ShapeDtypeStruct((3, CZ, CX, CY), F32)
    hbm, vmem = pl.BlockSpec(memory_space=pltpu.HBM), pl.BlockSpec(memory_space=pltpu.VMEM)
    dma = pltpu.SemaphoreType.DMA
    parts = (
        (3, CZ, CX, CY),
        (3, CZ + 3, CX, CY),
        (3, 16, CY),
        (3, 24, CY),
        (24, CY),
        (CZ + 2, CX, CY),
        (CZ + 1, CX, CY),
        (CZ, CX, CY),
        (3, CX, CY),
        grid.shape,
    )
    fields = pl.pallas_call(
        kernel,
        out_shape=[pltpu.VMEM(part, F32) for part in parts],
        in_specs=[hbm] * 12,
        out_specs=[vmem] * len(parts),
        scratch_shapes=[
            pltpu.VMEM((1, OV), jnp.int32),
            pltpu.VMEM((1, OV), jnp.int32),
            pltpu.VMEM((1, OV), jnp.int32),
            pltpu.VMEM((3, 4, 128), F32),
            pltpu.VMEM((4, CX), jnp.int32),
            pltpu.VMEM((4, CX), jnp.int32),
            pltpu.VMEM((3, CZ + 6, 32, CY), F32),
            pltpu.VMEM((3, CZ + 6, 32, CY), F32),
            pltpu.VMEM((COMPS, NBLK, 128), F32),
            pltpu.VMEM((NBLK, 128), F32),
            pltpu.VMEM((CZ, CX, CY), F32),
            pltpu.VMEM((3, CZ, CX, CY), F32),
            pltpu.VMEM((CZ, CX, CY), F32),
            pltpu.VMEM((GROUPS, ROWS, OV), BF16),
            pltpu.VMEM((2 * NBLK, 256), BF16),
            pltpu.VMEM((COMPS, N_TILE * CAP, 128), F32),
            pltpu.VMEM((COMPS, TX - 1, CAP * (TY - 1), 128), F32),
            pltpu.VMEM((COMPS, RROWS, 128), F32),
            pltpu.VMEM((N_TILE, 1, 128), F32),
            pltpu.VMEM((TX - 1, TY - 1, 1, 128), F32),
            pltpu.VMEM((N_TILE, 1, 128), F32),
            pltpu.VMEM((NBLK, RROWS), BF16),
            pltpu.VMEM((2, 8 * len(PLANES), CY), F32),
            pltpu.VMEM((8 * len(PLANES), CY), F32),
            pltpu.VMEM((8 * len(PLANES), CY), F32),
            pltpu.VMEM((4, len(LINES), 1, CY), F32),
            pltpu.VMEM((4, len(LINES), 1, CY), F32),
            pltpu.VMEM((N_TILE, 3, 4, 128), F32),
            pltpu.VMEM((3, 16, CY), F32),
            pltpu.VMEM((8, CY), F32),
            pltpu.VMEM((8, CY), F32),
            pltpu.VMEM((3, 3, 1, CY), F32),
            pltpu.VMEM((3, 3, 1, CY), F32),
            dma((6,)),
            dma((6,)),
            dma((1,)),
            dma((COMPS,)),
            dma((COMPS - 1 + len(PARTS),)),
            dma((COMPS, TX - 1)),
            dma((COMPS,)),
            dma,
            dma,
            dma,
            dma((TX - 1,)),
            dma((8,)),
            dma((8,)),
            dma((TY - 1,)),
            dma((TY - 1,)),
            dma((TX - 1,)),
            dma((TX - 1,)),
            dma((16,)),
            dma((16,)),
        ],
        compiler_params=pltpu.CompilerParams(
            collective_id=0, has_side_effects=True, vmem_limit_bytes=48 * 2**20
        ),
    )(
        *(
            pltpu.with_memory_space_constraint(value, pltpu.HBM)
            for value in (
                displacement,
                old_mass,
                old_momentum.transpose(1, 0, 2),
                intersection_fraction,
                entry_order,
                target_owner.reshape(1, OV),
                target_block.reshape(1, OV),
                kept_mass,
                kept_momentum,
                surface_panels.transpose(1, 0, 2),
                panel_ids[0].T,
                contact_flags[0].T,
            )
        )
    )
    return pl.pallas_call(
        finish,
        out_shape=(grid, grid),
        in_specs=[vmem] * len(parts),
        out_specs=(hbm, hbm),
        scratch_shapes=[pltpu.VMEM(grid.shape, F32), dma((CZ + 2,))],
        compiler_params=pltpu.CompilerParams(vmem_limit_bytes=4 * 2**20),
    )(*(pltpu.with_memory_space_constraint(field, pltpu.VMEM) for field in fields))


def solution(mesh):
    return jax.shard_map(
        shards,
        mesh=mesh,
        in_specs=(
            P(None, "band", "tile", None),
            P(("band", "tile"), None),
            P(("band", "tile"), None, None),
            P(("band", "tile"), None),
            P(("band", "tile"), None),
            P(("band", "tile"), None),
            P(("band", "tile")),
            P("band", "tile", None),
            P(None, "band", "tile", None),
            P(("band", "tile"), None, None),
            P("band", "tile", None),
            P("band", "tile", None),
        ),
        out_specs=(P(None, "band", "tile", None), P(None, "band", "tile", None)),
        check_vma=False,
    )
```
